128 devices in a mesh: pixel: 8 (over x, z_lo), date: 16 (over z_hi, y, core).
Axes of the slice: x: 4, y: 4, z: 4 (z_hi: 2, z_lo: 2; z = z_hi * 2 + z_lo), core: 2. Of those that a mesh axis runs over, the one named last changes fastest.
Arguments:
- raw_echoes: bfloat16 [2, 2048, 4096], P(None, ('pixel', 'date')), may hold values from -6 to 6
- range_phase: float32 [4096], replicated, may hold values from -3.140625 to 3.140625
- azimuth_phase: bfloat16 [4096, 2048], P('pixel'), may hold values from -3.140625 to 3.140625
- archive: bfloat16 [32, 2, 4096, 2048], P('date', None, 'pixel'), may hold values from -6 to 6
- date_order: int32 [32], P('date'), may hold values from 0 to 31, as said below
Outputs:
- coherence: float32 [32, 2, 1024, 128], P('date', None, 'pixel')
The draws below stay inside these ranges and needn't reach their ends.
Inputs may be any that keep to these rules, and one draw needn't show every extreme that they name: `date_order`: entry block b of 2 entries (positions b * 2 to (b + 1) * 2 - 1) holds each of the slots b * 2 to (b + 1) * 2 - 1 exactly once.
All inputs are finite; a program needn't handle non-finite values.
Results may differ from the reference program's by a relative error of at most 0.0041.
Values may be sent and summed in bfloat16 or wider, within the bound.
No kernel may reach another device: no remote copies, remote signals or barrier semaphores. Data moves between devices by JAX's collectives and lax.ppermute only.
A program may use at most 128 MiB of HBM per device.

```python
import jax
import jax.numpy as jnp
from jax import lax

R = 4096
A = 2048
LR = 4
LA = 16
D_LOC = 2
NDATES = 32


def draw_date_order(key, part):
    key = jax.random.fold_in(key, 7)
    block_count = NDATES // D_LOC

    def one_block(block_index):
        shuffled = jax.random.permutation(jax.random.fold_in(key, block_index), D_LOC)
        return block_index * D_LOC + shuffled.astype(jnp.int32)
    return jax.vmap(one_block)(jnp.arange(block_count, dtype=jnp.int32)).reshape(NDATES).astype(jnp.int32)


def levels(own_key, extent, pieces, low, high):
    def one(dim, parts):
        heights = jax.random.uniform(jax.random.fold_in(jax.random.fold_in(own_key, 6), dim), (parts,), jnp.float32, low / len(pieces), high / len(pieces))
        return jnp.repeat(jnp.exp(heights), extent[dim] // parts).reshape((-1,) + (1,) * (len(extent) - dim - 1))

    level = one(*pieces[0])
    for cut in pieces[1:]:
        level = level * one(*cut)
    return level


def scatter_about(rng, shape, spread, most, shards=(), kind=jnp.bfloat16):
    drawn = spread * jax.random.normal(rng, shape, jnp.float32)
    if shards:
        drawn = drawn * levels(rng, shape, shards, -0.22, 0.18)
    return jnp.clip(drawn, -most, most).astype(kind)


def setup_inputs(seed: int = 0) -> dict:
    arg_keys = jax.random.split(jax.random.key(seed), 6)
    raw_echoes = scatter_about(arg_keys[0], (2, A, R), 1.0, 6.0, ((1, 128),))
    range_phase = jnp.clip(jax.random.uniform(arg_keys[1], (R,), jnp.float32, -3.140625, 3.140625), -3.140625, 3.140625)
    azimuth_phase = jnp.clip(jax.random.uniform(arg_keys[2], (R, A), jnp.float32, -3.140625, 3.140625), -3.140625, 3.140625).astype(jnp.bfloat16)
    archive = scatter_about(arg_keys[3], (NDATES, 2, R, A), 1.0, 6.0, ((0, 16), (2, 8)))
    date_order = draw_date_order(jax.random.fold_in(arg_keys[5], 71), 0)
    return {"raw_echoes": raw_echoes, "range_phase": range_phase, "azimuth_phase": azimuth_phase, "archive": archive, "date_order": date_order}


def window_mean(values):
    rows, cols = (values.shape[-2], values.shape[-1])
    blocks = values.reshape(values.shape[:-2] + (rows // LR, LR, cols // LA, LA))
    return lax.optimization_barrier(jnp.mean(blocks, axis=(-3, -1)))

def reference(raw_echoes, range_phase, azimuth_phase, archive, date_order):
    echoes = raw_echoes[0].astype(jnp.float32) + 1j * raw_echoes[1].astype(jnp.float32)
    spectrum = jnp.fft.fft(echoes, axis=1, norm='ortho') * jnp.exp(1j * range_phase)[None, :]
    ranged = jnp.fft.ifft(spectrum, axis=1, norm='ortho')
    line_real = jnp.real(ranged).astype(jnp.bfloat16).astype(jnp.float32)
    line_imag = jnp.imag(ranged).astype(jnp.bfloat16).astype(jnp.float32)
    lines = line_real + 1j * line_imag
    az_angle = jnp.transpose(azimuth_phase.astype(jnp.float32))
    spectrum = jnp.fft.fft(lines, axis=0, norm='ortho') * jnp.exp(1j * az_angle)
    focused = jnp.fft.ifft(spectrum, axis=0, norm='ortho')
    new_real = jnp.transpose(jnp.real(focused)).astype(jnp.bfloat16).astype(jnp.float32)
    new_imag = jnp.transpose(jnp.imag(focused)).astype(jnp.bfloat16).astype(jnp.float32)
    power_new = window_mean(new_real * new_real + new_imag * new_imag)
    new_scale = lax.rsqrt(power_new + 1e-06)

    def one_date(stored):
        old_real = stored[0].astype(jnp.float32)
        old_imag = stored[1].astype(jnp.float32)
        cross_real = window_mean(new_real * old_real + new_imag * old_imag)
        cross_imag = window_mean(new_imag * old_real - new_real * old_imag)
        power_old = window_mean(old_real * old_real + old_imag * old_imag)
        scale = new_scale * lax.rsqrt(power_old + 1e-06)
        return jnp.stack([cross_real * scale, cross_imag * scale])
    normalized = lax.map(one_date, archive)
    return normalized[date_order]
```

```python
from functools import partial
import math

import jax
import jax.numpy as jnp
import numpy as np
from jax import lax
from jax.experimental import pallas as pl
from jax.experimental.pallas import tpu as pltpu
from jax.sharding import PartitionSpec as P

F32 = jnp.float32
BF16 = jnp.bfloat16
EPSILON = 1e-06
R = 4096
A = 2048
ROWS = 64
LINES = 16
VMEM_BYTES = 50 * 2**20
ALL = ("pixel", "date")
VMEM = pl.BlockSpec(memory_space=pltpu.VMEM)


def cmul(a, b):
    return (a[0] * b[0] - a[1] * b[1], a[0] * b[1] + a[1] * b[0])


def turned(value, k, n, sign):
    if k == 0:
        return value
    re, im = value
    if 8 * k == n:
        return ((re - im) * math.sqrt(0.5), (im + re) * math.sqrt(0.5)) if sign > 0 else (
            (re + im) * math.sqrt(0.5),
            (im - re) * math.sqrt(0.5),
        )
    if 8 * k == 3 * n:
        return ((re + im) * -math.sqrt(0.5), (re - im) * math.sqrt(0.5)) if sign > 0 else (
            (im - re) * math.sqrt(0.5),
            (re + im) * -math.sqrt(0.5),
        )
    angle = sign * 2.0 * math.pi * k / n
    return cmul(value, (math.cos(angle), math.sin(angle)))


def fft(values, sign):
    n = len(values)
    if n == 1:
        return values
    even, odd = fft(values[0::2], sign), fft(values[1::2], sign)
    low, high = [], []
    for k in range(n // 2):
        er, ei = even[k]
        if 4 * k == n:
            tr, ti = odd[k]
            plus, minus = (er - ti, ei + tr), (er + ti, ei - tr)
            low.append(plus if sign > 0 else minus)
            high.append(minus if sign > 0 else plus)
        else:
            tr, ti = turned(odd[k], k, n, sign)
            low.append((er + tr, ei + ti))
            high.append((er - tr, ei - ti))
    return low + high


def split(table):
    table = np.asarray(table, np.float32)
    high = table.astype(BF16)
    low = (table - high.astype(np.float32)).astype(BF16)
    return high, low


def real_form(angle, sign):
    c, s = np.cos(angle), sign * np.sin(angle)
    return np.block([[c, s], [-s, c]])


def range_tables():
    t = np.arange(128)
    angle = 2 * np.pi * np.outer(t, t) / 128
    fwd = np.concatenate(split(real_form(angle, -1)), axis=1)
    bwd = np.concatenate(split(real_form(angle, 1)), axis=1)
    twist = 2 * np.pi * np.outer(np.arange(32), t) / R
    return fwd, bwd, np.stack([np.cos(twist), -np.sin(twist)]).astype(np.float32)


def azimuth_tables():
    s = np.arange(128)
    fwd = np.concatenate(split(real_form(2 * np.pi * np.outer(s, s) / 128, -1).T), axis=1)
    k1 = np.arange(128)[:, None]
    i = np.arange(8)[None, :]
    t0 = np.exp(-2j * np.pi * i * k1 / A)
    t1 = np.exp(-2j * np.pi * (i + 8) * k1 / A)
    w = np.exp(-2j * np.pi * i / 16)
    here = np.stack([t0, -w * t1], axis=-1)
    there = np.stack([t1, w * t0], axis=-1)
    twist = np.stack([here.real, here.imag, there.real, there.imag])
    twist = np.repeat(twist, 64, axis=-1).reshape(4, 128, 8 * 128).astype(np.float32)
    k, lam = np.meshgrid(np.arange(8), np.arange(8), indexing="ij")
    m = (lam + 16 * k).reshape(64)
    beta = np.arange(128)
    columns = [real_form(2 * np.pi * np.outer(m + 8 * par, beta) / 128, 1) for par in (0, 1)]
    bwd_high, bwd_low = split(np.concatenate(columns, axis=1))
    bwd = np.stack([bwd_high, bwd_low])
    last = 2 * np.pi * np.outer(np.arange(16), beta) / A
    return fwd, twist, bwd, np.stack([np.cos(last), np.sin(last)]).astype(np.float32)


def pooling_table():
    return (np.arange(A)[:, None] // 16 == np.arange(128)[None, :]).astype(BF16)


def dot(a, b):
    return jnp.dot(a, b, preferred_element_type=F32)


def halves(x):
    high = x.astype(BF16)
    return high, (x - high.astype(F32)).astype(BF16)


def dot_split(x, table):
    high, low = halves(x)
    n = table.shape[1] // 2
    return dot(high, table[:, :n]) + dot(low, table[:, :n]) + dot(high, table[:, n:])


def range_kernel(raw, phase, twist, fwd, bwd, out, a, b):
    values = [
        (raw[0, :, 128 * q : 128 * q + 128].astype(F32), raw[1, :, 128 * q : 128 * q + 128].astype(F32))
        for q in range(32)
    ]
    for k0, value in enumerate(fft(values, -1)):
        re, im = cmul(value, (twist[0, k0 : k0 + 1, :], twist[1, k0 : k0 + 1, :]))
        a[16 * k0 : 16 * k0 + 16, 0:128] = re
        a[16 * k0 : 16 * k0 + 16, 128:256] = im
    b[...] = dot_split(a[...], fwd)
    angle = phase[...]
    cosine, sine = jnp.cos(angle) * (1.0 / R), jnp.sin(angle) * (1.0 / R)
    for k0 in range(32):
        rows = slice(16 * k0, 16 * k0 + 16)
        re, im = cmul((b[rows, 0:128], b[rows, 128:256]), (cosine[k0 : k0 + 1], sine[k0 : k0 + 1]))
        a[rows, 0:128] = re
        a[rows, 128:256] = im
    b[...] = dot_split(a[...], bwd)
    values = []
    for k0 in range(32):
        rows = slice(16 * k0, 16 * k0 + 16)
        values.append(
            cmul((b[rows, 0:128], b[rows, 128:256]), (twist[0, k0 : k0 + 1, :], -twist[1, k0 : k0 + 1, :]))
        )
    left = lax.broadcasted_iota(jnp.int32, (8, 128), 1) < 64
    for q, value in enumerate(fft(values, 1)):
        for half in range(2):
            parts = []
            for part in value:
                low, high = part[0:8], part[8:16]
                if half == 0:
                    parts.append(jnp.where(left, low, pltpu.roll(high, 64, 1)))
                else:
                    parts.append(jnp.where(left, pltpu.roll(low, 64, 1), high))
            message = jnp.concatenate(parts, axis=0).astype(BF16)
            pixel, core, block = q // 4, (q // 2) % 2, 2 * (q % 2) + half
            for zh in range(2):
                y = (block + 2 * zh) % 4
                out[pixel * 16 + zh * 8 + y * 2 + core] = message


def compress_range(raw, phase):
    fwd, bwd, twist = range_tables()
    return pl.pallas_call(
        range_kernel,
        out_shape=jax.ShapeDtypeStruct((128, 16, 128), BF16),
        in_specs=[VMEM] * 5,
        out_specs=VMEM,
        scratch_shapes=[pltpu.VMEM((512, 256), F32)] * 2,
        compiler_params=pltpu.CompilerParams(vmem_limit_bytes=VMEM_BYTES),
        cost_estimate=pl.CostEstimate(flops=4 * 10**8, bytes_accessed=2 * 10**6, transcendentals=8192),
        name="compress_range",
    )(raw, phase.reshape(128, 32).T, twist, fwd, bwd)


def phase_kernel(where, angle, out):
    for k in range(8):
        block = jnp.concatenate(
            [angle[:, 256 * k : 256 * k + 128], angle[:, 256 * k + 128 : 256 * k + 256]], axis=0
        )
        turned_block = block.astype(F32).T
        out[0, k] = jnp.cos(turned_block) * (1.0 / A)
        out[1, k] = jnp.sin(turned_block) * (1.0 / A)


def phase_factors(azimuth_phase, where):
    return pl.pallas_call(
        phase_kernel,
        out_shape=jax.ShapeDtypeStruct((2, 8, 128, 128), F32),
        grid_spec=pltpu.PrefetchScalarGridSpec(
            num_scalar_prefetch=1,
            grid=(1,),
            in_specs=[pl.BlockSpec((ROWS, A), lambda g, where: (where[0], 0))],
            out_specs=pl.BlockSpec((2, 8, 128, 128), lambda g, where: (0, 0, 0, 0)),
        ),
        compiler_params=pltpu.CompilerParams(vmem_limit_bytes=VMEM_BYTES),
        cost_estimate=pl.CostEstimate(flops=10**7, bytes_accessed=2 * 10**6, transcendentals=262144),
        name="phase_factors",
    )(where, azimuth_phase)


def focus_kernel(lines, factors, fwd, twist, bwd, last, out, wide, packed, spec, filtered, parts):
    wide[...] = lines[...].reshape(2048, 128).astype(F32)
    for j in range(16):
        ri, i = j // 8, j % 8
        packed[128 * ri : 128 * ri + 128, 128 * i : 128 * i + 128] = wide[pl.ds(j, 128, stride=16), :].astype(BF16)
    spec[...] = dot(fwd[:, 0:256], packed[...]) + dot(fwd[:, 256:512], packed[...])

    def tile(step, carry):
        rows = pl.ds(pl.multiple_of(step * 8, 8), 8)
        below = pl.ds(pl.multiple_of(step * 8 + 128, 8), 8)
        values = []
        for i in range(8):
            lanes = slice(128 * i, 128 * i + 128)
            value = (spec[rows, lanes], spec[below, lanes])
            other = (pltpu.roll(value[0], 64, 1), pltpu.roll(value[1], 64, 1))
            a = cmul(value, (twist[0, rows, lanes], twist[1, rows, lanes]))
            b = cmul(other, (twist[2, rows, lanes], twist[3, rows, lanes]))
            values.append((a[0] + b[0], a[1] + b[1]))
        for k, value in enumerate(fft(values, -1)):
            re, im = cmul(value, (factors[0, k, rows, :], factors[1, k, rows, :]))
            filtered[0, k, rows, :] = re
            filtered[1, k, rows, :] = im
        return carry

    lax.fori_loop(0, 16, tile, 0)

    for kappa in range(16):
        block = jnp.concatenate(
            [filtered[ri, k, pl.ds(kappa, 8, stride=16), :] for ri in range(2) for k in range(8)], axis=0
        )
        high, low = halves(block.T)
        both = dot(high, bwd[0]) + dot(low, bwd[0]) + dot(high, bwd[1])
        summed = both[0:64, 0:256] + both[64:128, 256:512]
        re, im = cmul(
            (summed[:, 0:128], summed[:, 128:256]),
            (last[0, kappa : kappa + 1, :], last[1, kappa : kappa + 1, :]),
        )
        parts[0, kappa] = re
        parts[1, kappa] = im

    def rows_out(step, carry):
        rows = pl.ds(pl.multiple_of(step * 16, 16), 16)
        values = [(parts[0, kappa, rows, :], parts[1, kappa, rows, :]) for kappa in range(16)]
        for alpha, (re, im) in enumerate(fft(values, 1)):
            lanes = slice(128 * alpha, 128 * alpha + 128)
            out[0, rows, lanes] = re.astype(BF16)
            out[1, rows, lanes] = im.astype(BF16)
        return carry

    lax.fori_loop(0, 4, rows_out, 0)


def focus_columns(lines, factors):
    fwd, twist, bwd, last = azimuth_tables()
    return pl.pallas_call(
        focus_kernel,
        out_shape=jax.ShapeDtypeStruct((2, ROWS, A), BF16),
        in_specs=[VMEM] * 6,
        out_specs=VMEM,
        scratch_shapes=[
            pltpu.VMEM((2048, 128), F32),
            pltpu.VMEM((256, 1024), BF16),
            pltpu.VMEM((256, 1024), F32),
            pltpu.VMEM((2, 8, 128, 128), F32),
            pltpu.VMEM((2, 16, ROWS, 128), F32),
        ],
        compiler_params=pltpu.CompilerParams(vmem_limit_bytes=VMEM_BYTES),
        cost_estimate=pl.CostEstimate(flops=10**9, bytes_accessed=4 * 10**6, transcendentals=0),
        name="focus_columns",
    )(lines, factors, fwd, twist, bwd, last)


def window_rows(pooled, row_count):
    return sum(pooled[pl.ds(j, row_count // 4, stride=4), :] for j in range(4))


def old_kernel(archive, pooling, out, pooled):
    for date in range(2):
        total = jnp.zeros((ROWS, 128), F32)
        for chunk in range(8):
            lanes = slice(256 * chunk, 256 * chunk + 256)
            re, im = archive[date, 0, :, lanes].astype(F32), archive[date, 1, :, lanes].astype(F32)
            high, low = halves(re * re + im * im)
            total += dot(high, pooling[lanes, :]) + dot(low, pooling[lanes, :])
        pooled[ROWS * date : ROWS * date + ROWS, :] = total
    scale = lax.rsqrt(window_rows(pooled, 2 * ROWS) * (1.0 / 64) + EPSILON)
    out[...] = scale.reshape(2, 16, 128)


def old_scales(archive):
    return pl.pallas_call(
        old_kernel,
        out_shape=jax.ShapeDtypeStruct((2, 128, 128), F32),
        grid=(8,),
        in_specs=[pl.BlockSpec((2, 2, ROWS, A), lambda g: (0, 0, g, 0)), VMEM],
        out_specs=pl.BlockSpec((2, 16, 128), lambda g: (0, g, 0)),
        scratch_shapes=[pltpu.VMEM((2 * ROWS, 128), F32)],
        compiler_params=pltpu.CompilerParams(vmem_limit_bytes=VMEM_BYTES),
        cost_estimate=pl.CostEstimate(flops=10**9, bytes_accessed=9 * 10**6, transcendentals=0),
        name="old_scales",
    )(archive, pooling_table())


def cross_block(image, archives, pooling, pooled):
    total = [jnp.zeros((2 * ROWS, 128), F32) for _ in range(4)]
    power = jnp.zeros((ROWS, 128), F32)
    for chunk in range(8):
        lanes = slice(256 * chunk, 256 * chunk + 256)
        new_re, new_im = image[0, :, lanes].astype(F32), image[1, :, lanes].astype(F32)
        pool = pooling[lanes, :]
        power += dot((new_re * new_re + new_im * new_im).astype(BF16), pool)
        for date in range(4):
            old = archives[date // 2]
            old_re, old_im = old[date % 2, 0, :, lanes].astype(F32), old[date % 2, 1, :, lanes].astype(F32)
            real = new_re * old_re + new_im * old_im
            imag = new_im * old_re - new_re * old_im
            total[date] += dot(jnp.concatenate([real, imag], axis=0).astype(BF16), pool)
    for date in range(4):
        pooled[2 * ROWS * date : 2 * ROWS * (date + 1), :] = total[date]
    pooled[8 * ROWS : 9 * ROWS, :] = power
    sums = window_rows(pooled, 9 * ROWS) * (1.0 / 64)
    scale = lax.rsqrt(sums[128:144] + EPSILON)
    return sums[0:128].reshape(2, 2, 2, 16, 128) * scale


def first_kernel(where, image, own, other, pooling, own_out, other_out, pooled):
    result = cross_block(image, (own, other), pooling, pooled)
    own_out[...] = result[0]
    other_out[...] = result[1]


def rest_kernel(where, image1, image2, image3, own, other, pooling, own_first, other_first, own_out, other_out, pooled):
    step = pl.program_id(0)

    def put(block, own_part, other_part):
        rows = pl.ds(pl.multiple_of(block * 16, 16), 16)
        own_out[:, :, rows, :] = own_part
        other_out[:, :, rows, :] = other_part

    @pl.when(step == 0)
    def _():
        put(where[4], own_first[...], other_first[...])

    for n, image in enumerate((image1, image2, image3)):

        @pl.when(step == n)
        def _(n=n, image=image):
            result = cross_block(image, (own, other), pooling, pooled)
            put(where[5 + n], result[0], result[1])


def archive_spec(offset):
    return pl.BlockSpec((2, 2, ROWS, A), lambda g, where: (0, 0, where[g + offset], 0))


CROSS_PARAMS = dict(compiler_params=pltpu.CompilerParams(vmem_limit_bytes=VMEM_BYTES))


def cross_first(where, image, own, other):
    part = jax.ShapeDtypeStruct((2, 2, 16, 128), F32)
    return pl.pallas_call(
        first_kernel,
        out_shape=(part, part),
        grid_spec=pltpu.PrefetchScalarGridSpec(
            num_scalar_prefetch=1,
            grid=(1,),
            in_specs=[VMEM, archive_spec(0), archive_spec(0), VMEM],
            out_specs=(VMEM, VMEM),
            scratch_shapes=[pltpu.VMEM((9 * ROWS, 128), F32)],
        ),
        cost_estimate=pl.CostEstimate(flops=10**9, bytes_accessed=3 * 10**6, transcendentals=0),
        name="cross_first",
        **CROSS_PARAMS,
    )(where, image, own, other, pooling_table())


def cross_rest(where, images, own, other, first):
    whole = jax.ShapeDtypeStruct((2, 2, 64, 128), F32)
    return pl.pallas_call(
        rest_kernel,
        out_shape=(whole, whole),
        grid_spec=pltpu.PrefetchScalarGridSpec(
            num_scalar_prefetch=1,
            grid=(3,),
            in_specs=[VMEM] * 3 + [archive_spec(1), archive_spec(1)] + [VMEM] * 3,
            out_specs=(VMEM, VMEM),
            scratch_shapes=[pltpu.VMEM((9 * ROWS, 128), F32)],
        ),
        cost_estimate=pl.CostEstimate(flops=3 * 10**9, bytes_accessed=9 * 10**6, transcendentals=0),
        name="cross_rest",
        **CROSS_PARAMS,
    )(where, *images, own, other, pooling_table(), *first)


def final_kernel(where, order, mine, received, scales, out):
    core, first_slot = where[8], where[9]
    for rows, source in ((core, mine), (1 - core, received)):
        rows = pl.ds(pl.multiple_of(rows * 64, 64), 64)
        for n in range(2):
            slot = order[n] - first_slot
            out[n, :, rows, :] = source[slot] * scales[slot, rows, :]


def assemble(where, date_order, mine, received, scales):
    return pl.pallas_call(
        final_kernel,
        out_shape=jax.ShapeDtypeStruct((2, 2, 128, 128), F32),
        in_specs=[pl.BlockSpec(memory_space=pltpu.SMEM)] * 2 + [VMEM] * 3,
        out_specs=VMEM,
        cost_estimate=pl.CostEstimate(flops=10**6, bytes_accessed=10**6, transcendentals=0),
        name="assemble",
    )(where, date_order, mine, received, scales)


def pairs(step):
    out = []
    for date in range(16):
        zh, y, core = step(date // 8, date // 2 % 4, date % 2)
        out.append((date, zh * 8 + y % 4 * 2 + core))
    return out


OTHER_CORE = pairs(lambda zh, y, core: (zh, y, 1 - core))
OTHER_Z = pairs(lambda zh, y, core: (1 - zh, y, core))
NEXT_Y = pairs(lambda zh, y, core: (zh, y + 1, core))
LAST_Y = pairs(lambda zh, y, core: (zh, y + 3, core))


def on_device(raw_echoes, range_phase, azimuth_phase, archive, date_order):
    date = lax.axis_index("date")
    zh, y, core = date // 8, date // 2 % 4, date % 2
    block = (y + 2 * zh) % 4
    blocks = jnp.stack([block, (block + 2) % 4, (block + 3) % 4, (block + 1) % 4])
    where = jnp.concatenate([core * 4 + blocks, blocks, jnp.stack([core, date * 2])]).astype(jnp.int32)

    messages = compress_range(raw_echoes, range_phase)
    messages, azimuth_phase, archive = lax.optimization_barrier((messages, azimuth_phase, archive))
    lines = lax.all_to_all(messages, ALL, 0, 0, tiled=True)
    other_archive = lax.ppermute(archive, "date", OTHER_CORE)
    factors = phase_factors(azimuth_phase, where)
    scales = old_scales(archive)
    image = focus_columns(lines, factors)
    images = [lax.ppermute(image, "date", perm) for perm in (OTHER_Z, NEXT_Y, LAST_Y)]
    first = cross_first(where, image, archive, other_archive)
    mine, others = cross_rest(where, images, archive, other_archive, first)
    received = lax.ppermute(others, "date", OTHER_CORE)
    return assemble(where, date_order, mine, received, scales)


def solution(mesh):
    return jax.shard_map(
        on_device,
        mesh=mesh,
        in_specs=(P(None, ALL, None), P(), P("pixel", None), P("date", None, "pixel", None), P("date")),
        out_specs=P("date", None, "pixel", None),
        check_vma=False,
    )
```

```python
import math

import jax
import jax.numpy as jnp
import numpy as np
from jax import lax
from jax.experimental import pallas as pl
from jax.experimental.pallas import tpu as pltpu
from jax.sharding import PartitionSpec as P

F32 = jnp.float32
BF16 = jnp.bfloat16
EPSILON = 1e-06
R = 4096
A = 2048
ROWS = 64
LINES = 16
ALL = ("pixel", "date")
VMEM = pl.BlockSpec(memory_space=pltpu.VMEM)
SMEM = pl.BlockSpec(memory_space=pltpu.SMEM)
HBM = pl.BlockSpec(memory_space=pltpu.HBM)


def cmul(a, b):
    return (a[0] * b[0] - a[1] * b[1], a[0] * b[1] + a[1] * b[0])


def turned(value, k, n, sign):
    if k == 0:
        return value
    re, im = value
    if 8 * k == n:
        return ((re - im) * math.sqrt(0.5), (im + re) * math.sqrt(0.5)) if sign > 0 else (
            (re + im) * math.sqrt(0.5),
            (im - re) * math.sqrt(0.5),
        )
    if 8 * k == 3 * n:
        return ((re + im) * -math.sqrt(0.5), (re - im) * math.sqrt(0.5)) if sign > 0 else (
            (im - re) * math.sqrt(0.5),
            (re + im) * -math.sqrt(0.5),
        )
    angle = sign * 2.0 * math.pi * k / n
    return cmul(value, (math.cos(angle), math.sin(angle)))


def fft(values, sign):
    n = len(values)
    if n == 1:
        return values
    even, odd = fft(values[0::2], sign), fft(values[1::2], sign)
    low, high = [], []
    for k in range(n // 2):
        er, ei = even[k]
        if 4 * k == n:
            tr, ti = odd[k]
            plus, minus = (er - ti, ei + tr), (er + ti, ei - tr)
            low.append(plus if sign > 0 else minus)
            high.append(minus if sign > 0 else plus)
        else:
            tr, ti = turned(odd[k], k, n, sign)
            low.append((er + tr, ei + ti))
            high.append((er - tr, ei - ti))
    return low + high


def split(table):
    table = np.asarray(table, np.float32)
    high = table.astype(BF16)
    low = (table - high.astype(np.float32)).astype(BF16)
    return high, low


def real_form(angle, sign):
    c, s = np.cos(angle), sign * np.sin(angle)
    return np.block([[c, s], [-s, c]])


def range_tables():
    t = np.arange(128)
    k1 = 4 * (t % 32) + t // 32
    angle = 2 * np.pi * np.outer(t, k1) / 128
    fwd = np.concatenate(split(real_form(angle, -1)), axis=1)
    bwd = np.concatenate(split(real_form(angle.T, 1)), axis=1)
    twist = 2 * np.pi * np.outer(np.arange(32), t) / R
    return np.stack([np.cos(twist), -np.sin(twist)]).astype(np.float32), fwd, bwd


def azimuth_tables():
    s = np.arange(128)
    fwd = np.concatenate(split(real_form(2 * np.pi * np.outer(s, s) / 128, -1).T), axis=1)
    k1 = np.arange(128)[:, None]
    i = np.arange(8)[None, :]
    twist = np.stack([np.exp(-2j * np.pi * (i + 8 * half) * k1 / A) for half in (0, 1)], axis=-1)
    twist = np.repeat(np.stack([twist.real, twist.imag]), 64, axis=-1).transpose(0, 2, 1, 3).astype(np.float32)
    odd = np.exp(-2j * np.pi * np.arange(8)[:, None] / 16 * (np.arange(128)[None, :] // 64))
    k, lam = np.meshgrid(np.arange(8), np.arange(8), indexing="ij")
    m = (lam + 16 * k).reshape(64)
    beta = np.arange(128)
    parts = [real_form(2 * np.pi * np.outer(m + 8 * par, beta) / 128, 1) for par in (0, 1)]
    bwd = np.concatenate(split(np.concatenate(parts, axis=0)), axis=1)
    last = 2 * np.pi * np.outer(np.arange(16), beta) / A
    rows = np.concatenate([np.exp(1j * last), odd], axis=0)
    rows = np.stack([rows.real, rows.imag]).astype(np.float32)
    return twist, np.concatenate([fwd, bwd], axis=0), rows


def pooling_table():
    return (np.arange(A)[:, None] // 16 == np.arange(128)[None, :]).astype(BF16)


def dot(a, b):
    return jnp.dot(a, b, preferred_element_type=F32)


def halves(x):
    high = x.astype(BF16)
    return high, (x - high.astype(F32)).astype(BF16)


def dot_split(x, table):
    high, low = halves(x)
    n = table.shape[1] // 2
    return dot(high, table[:, :n]) + dot(low, table[:, :n]) + dot(high, table[:, n:])


def params(mib):
    return pltpu.CompilerParams(vmem_limit_bytes=mib * 2**20)


def cost(flops, moved, transcendentals=0):
    return pl.CostEstimate(flops=flops, bytes_accessed=moved, transcendentals=transcendentals)


def in_hbm(*arrays):
    return [pltpu.with_memory_space_constraint(x, pltpu.HBM) for x in arrays]


def in_vmem(*arrays):
    return [pltpu.with_memory_space_constraint(x, pltpu.VMEM) for x in arrays]


def fetch(sources, targets, sems):
    copies = [
        pltpu.make_async_copy(source, target, sems.at[n]) for n, (source, target) in enumerate(zip(sources, targets))
    ]
    for copy in copies:
        copy.start()
    return copies


def range_kernel(raw_hbm, phase_hbm, twist_hbm, fwd_hbm, bwd_hbm, out, raw, phase, twist, fwd, bwd, a, b, sems):
    copies = fetch(
        (phase_hbm, raw_hbm, twist_hbm, fwd_hbm, bwd_hbm), (phase, raw, twist, fwd, bwd), sems
    )
    copies[0].wait()
    angle = phase[...]
    angle = jnp.concatenate(
        [angle] + [pltpu.roll(angle, 128 - 32 * g, 1) for g in range(1, 4)], axis=0
    ).T[0:32]
    cosine, sine = jnp.cos(angle) * (1.0 / R), jnp.sin(angle) * (1.0 / R)
    copies[1].wait()
    copies[2].wait()
    values = [
        (raw[0, :, 128 * q : 128 * q + 128].astype(F32), raw[1, :, 128 * q : 128 * q + 128].astype(F32))
        for q in range(32)
    ]
    for k0, value in enumerate(fft(values, -1)):
        re, im = cmul(value, (twist[0, k0 : k0 + 1, :], twist[1, k0 : k0 + 1, :]))
        a[16 * k0 : 16 * k0 + 16, 0:128] = re
        a[16 * k0 : 16 * k0 + 16, 128:256] = im
    copies[3].wait()
    b[...] = dot_split(a[...], fwd)
    for k0 in range(32):
        rows = slice(16 * k0, 16 * k0 + 16)
        re, im = cmul((b[rows, 0:128], b[rows, 128:256]), (cosine[k0 : k0 + 1], sine[k0 : k0 + 1]))
        a[rows, 0:128] = re
        a[rows, 128:256] = im
    copies[4].wait()
    b[...] = dot_split(a[...], bwd)
    values = []
    for k0 in range(32):
        rows = slice(16 * k0, 16 * k0 + 16)
        values.append(
            cmul((b[rows, 0:128], b[rows, 128:256]), (twist[0, k0 : k0 + 1, :], -twist[1, k0 : k0 + 1, :]))
        )
    left = lax.broadcasted_iota(jnp.int32, (8, 128), 1) < 64
    for q, value in enumerate(fft(values, 1)):
        for half in range(2):
            parts = []
            for part in value:
                low, high = part[0:8], part[8:16]
                if half == 0:
                    parts.append(jnp.where(left, low, pltpu.roll(high, 64, 1)))
                else:
                    parts.append(jnp.where(left, pltpu.roll(low, 64, 1), high))
            message = jnp.concatenate(parts, axis=0).astype(BF16)
            pixel, core, block = q // 4, (q // 2) % 2, 2 * (q % 2) + half
            for zh in range(2):
                y = (block + 2 * zh) % 4
                out[pixel * 16 + zh * 8 + y * 2 + core] = message


def compress_range(raw, phase):
    twist, fwd, bwd = range_tables()
    return pl.pallas_call(
        range_kernel,
        out_shape=jax.ShapeDtypeStruct((128, 16, 128), BF16),
        in_specs=[HBM] * 5,
        out_specs=VMEM,
        scratch_shapes=[
            pltpu.VMEM((2, 16, R), BF16),
            pltpu.VMEM((32, 128), F32),
            pltpu.VMEM((2, 32, 128), F32),
            pltpu.VMEM((256, 512), BF16),
            pltpu.VMEM((256, 512), BF16),
            pltpu.VMEM((512, 256), F32),
            pltpu.VMEM((512, 256), F32),
            pltpu.SemaphoreType.DMA((5,)),
        ],
        compiler_params=params(24),
        cost_estimate=cost(4 * 10**8, 2 * 10**6, 8192),
        name="compress_range",
    )(*in_hbm(raw, phase.reshape(32, 128), *map(jnp.asarray, (twist, fwd, bwd))))


def prepare_kernel(
    where, angle_hbm, twist_hbm, mats_hbm, last_hbm, factors, mats, last, angle, sems
):
    rows = pl.ds(pl.multiple_of(where[0] * ROWS, ROWS), ROWS)
    copies = fetch(
        (angle_hbm.at[rows], twist_hbm, mats_hbm, last_hbm),
        (angle, factors.at[2:4], mats, last),
        sems,
    )
    copies[0].wait()
    for k in range(8):
        block = jnp.concatenate(
            [angle[:, 256 * k : 256 * k + 128], angle[:, 256 * k + 128 : 256 * k + 256]], axis=0
        )
        turned_block = block.astype(F32).T
        factors[0, k] = jnp.cos(turned_block) * (1.0 / A)
        factors[1, k] = jnp.sin(turned_block) * (1.0 / A)
    for copy in copies[1:]:
        copy.wait()


def prepare(azimuth_phase, where):
    tables = azimuth_tables()
    return pl.pallas_call(
        prepare_kernel,
        out_shape=(pltpu.VMEM((4, 8, 128, 128), F32), *(pltpu.VMEM(t.shape, t.dtype) for t in tables[1:])),
        in_specs=[SMEM] + [HBM] * 4,
        out_specs=(VMEM,) * 3,
        scratch_shapes=[pltpu.VMEM((ROWS, A), BF16), pltpu.SemaphoreType.DMA((4,))],
        compiler_params=params(24),
        cost_estimate=cost(10**7, 8 * 10**6, 262144),
        name="prepare",
    )(where, *in_hbm(azimuth_phase, *map(jnp.asarray, tables)))


def focus_kernel(lines, factors, mats, last, out, wide, packed, spec, filtered, turned_rows, parts):
    wide[...] = lines[...].reshape(2048, 128).astype(F32)
    for j in range(16):
        ri, i = j // 8, j % 8
        packed[128 * ri : 128 * ri + 128, 128 * i : 128 * i + 128] = wide[pl.ds(j, 128, stride=16), :].astype(BF16)
    spec[...] = dot(mats[0:256, 0:256], packed[...]) + dot(mats[0:256, 256:512], packed[...])

    sign = jnp.where(lax.broadcasted_iota(jnp.int32, (8, 128), 1) < 64, 1.0, -1.0)

    def tile(step, carry):
        rows = pl.ds(pl.multiple_of(step * 8, 8), 8)
        below = pl.ds(pl.multiple_of(step * 8 + 128, 8), 8)
        values = []
        for i in range(8):
            lanes = slice(128 * i, 128 * i + 128)
            value = cmul((spec[rows, lanes], spec[below, lanes]), (factors[2, i, rows, :], factors[3, i, rows, :]))
            value = tuple(pltpu.roll(part, 64, 1) + part * sign for part in value)
            if i:
                value = cmul(value, (last[0, 16 + i : 17 + i, :], last[1, 16 + i : 17 + i, :]))
            values.append(value)
        for k, value in enumerate(fft(values, -1)):
            re, im = cmul(value, (factors[0, k, rows, :], factors[1, k, rows, :]))
            filtered[0, k, rows, :] = re
            filtered[1, k, rows, :] = im
        return carry

    lax.fori_loop(0, 16, tile, 0, unroll=4)

    for kappa in range(16):
        block = jnp.concatenate(
            [filtered[ri, k, pl.ds(kappa, 8, stride=16), :] for ri in range(2) for k in range(8)], axis=0
        )
        block = block.T.astype(BF16)
        turned_rows[64 * kappa : 64 * kappa + 64, 0:128] = block[0:64]
        turned_rows[64 * kappa : 64 * kappa + 64, 128:256] = block[64:128]
    parts[...] = dot(turned_rows[...], mats[256:512, 0:256]) + dot(turned_rows[...], mats[256:512, 256:512])

    def rows_out(step, carry):
        rows = pl.ds(pl.multiple_of(step * 16, 16), 16)
        values = []
        for kappa in range(16):
            here = pl.ds(pl.multiple_of(step * 16 + 64 * kappa, 16), 16)
            values.append(
                cmul(
                    (parts[here, 0:128], parts[here, 128:256]),
                    (last[0, kappa : kappa + 1, :], last[1, kappa : kappa + 1, :]),
                )
            )
        for alpha, (re, im) in enumerate(fft(values, 1)):
            lanes = slice(128 * alpha, 128 * alpha + 128)
            out[0, rows, lanes] = re.astype(BF16)
            out[1, rows, lanes] = im.astype(BF16)
        return carry

    lax.fori_loop(0, 4, rows_out, 0, unroll=2)


def focus_columns(lines, factors, mats, last):
    return pl.pallas_call(
        focus_kernel,
        out_shape=jax.ShapeDtypeStruct((2, ROWS, A), BF16),
        in_specs=[VMEM] * 4,
        out_specs=VMEM,
        scratch_shapes=[
            pltpu.VMEM((2048, 128), F32),
            pltpu.VMEM((256, 1024), BF16),
            pltpu.VMEM((256, 1024), F32),
            pltpu.VMEM((2, 8, 128, 128), F32),
            pltpu.VMEM((1024, 256), BF16),
            pltpu.VMEM((1024, 256), F32),
        ],
        compiler_params=params(24),
        cost_estimate=cost(10**9, 4 * 10**6),
        name="focus_columns",
    )(lines, factors, mats, last)


def window_rows(pooled, row_count):
    return sum(pooled[pl.ds(j, row_count // 4, stride=4), :] for j in range(4)) * (1.0 / 64)


def old_kernel(archive, pooling, out, products, pooled):
    for date in range(2):
        for chunk in range(8):
            lanes = slice(256 * chunk, 256 * chunk + 256)
            re, im = archive[date, 0, :, lanes], archive[date, 1, :, lanes]
            products[ROWS * date : ROWS * date + ROWS, lanes] = re * re + im * im
    pooled[...] = dot(products[...], pooling[...])
    out[...] = lax.rsqrt(window_rows(pooled, 2 * ROWS) + EPSILON).reshape(2, 16, 128)


def old_scales(archive, pooling):
    return pl.pallas_call(
        old_kernel,
        out_shape=jax.ShapeDtypeStruct((2, 128, 128), F32),
        grid=(8,),
        in_specs=[
            pl.BlockSpec((2, 2, ROWS, A), lambda g: (0, 0, g, 0)),
            pl.BlockSpec((A, 128), lambda g: (0, 0)),
        ],
        out_specs=pl.BlockSpec((2, 16, 128), lambda g: (0, g, 0)),
        scratch_shapes=[pltpu.VMEM((2 * ROWS, A), BF16), pltpu.VMEM((2 * ROWS, 128), F32)],
        compiler_params=params(24),
        cost_estimate=cost(10**9, 9 * 10**6),
        name="old_scales",
    )(*in_hbm(archive, pooling))


def cross_products(products, row, image, old, old_rows):
    for chunk in range(8):
        lanes = slice(256 * chunk, 256 * chunk + 256)
        new_re, new_im = image[0, :, lanes], image[1, :, lanes]
        old_re, old_im = old[0, old_rows, lanes], old[1, old_rows, lanes]
        products[row : row + ROWS, lanes] = new_re * old_re + new_im * old_im
        products[row + ROWS : row + 2 * ROWS, lanes] = new_im * old_re - new_re * old_im


def power_products(products, row, image):
    for chunk in range(8):
        lanes = slice(256 * chunk, 256 * chunk + 256)
        new_re, new_im = image[0, :, lanes], image[1, :, lanes]
        products[row : row + ROWS, lanes] = new_re * new_re + new_im * new_im


ALL_ROWS = slice(0, ROWS)


def first_kernel(
    where, image, own, other, pooling_hbm, own_out, other_out, held, pooling, here, products, pooled, sems
):
    copies = []
    for n in range(4):
        rows = pl.ds(pl.multiple_of(where[n] * ROWS, ROWS), ROWS)
        for m, source in enumerate((own, other)):
            if n == 0:
                target = here.at[2 * m : 2 * m + 2]
            else:
                target = held.at[2 * m : 2 * m + 2, :, ROWS * (n - 1) : ROWS * n]
            copies.append(pltpu.make_async_copy(source.at[:, :, rows], target, sems.at[2 * n + m]))
            copies[-1].start()
    copies.insert(2, pltpu.make_async_copy(pooling_hbm, pooling, sems.at[8]))
    copies[2].start()
    power_products(products, 8 * ROWS, image)
    copies[0].wait()
    copies[1].wait()
    for date in range(4):
        cross_products(products, 2 * ROWS * date, image, here.at[date], ALL_ROWS)
    copies[2].wait()
    pooled[...] = dot(products[...], pooling[...])
    sums = window_rows(pooled, 9 * ROWS)
    result = sums[0:128].reshape(2, 2, 2, 16, 128) * lax.rsqrt(sums[128:144] + EPSILON)
    own_out[...] = result[0]
    other_out[...] = result[1]
    for copy in copies[3:]:
        copy.wait()


def cross_first(where, image, own, other, pooling):
    part = jax.ShapeDtypeStruct((2, 2, 16, 128), F32)
    return pl.pallas_call(
        first_kernel,
        out_shape=(part, part, pltpu.VMEM((4, 2, 3 * ROWS, A), BF16), pltpu.VMEM((A, 128), BF16)),
        in_specs=[SMEM, VMEM, HBM, HBM, HBM],
        out_specs=(VMEM,) * 4,
        scratch_shapes=[
            pltpu.VMEM((4, 2, ROWS, A), BF16),
            pltpu.VMEM((9 * ROWS, A), BF16),
            pltpu.VMEM((9 * ROWS, 128), F32),
            pltpu.SemaphoreType.DMA((9,)),
        ],
        compiler_params=params(24),
        cost_estimate=cost(10**9, 8 * 10**6),
        name="cross_first",
    )(where, image, *in_hbm(own, other, pooling))


def put(where, n, target, part):
    target[:, :, pl.ds(pl.multiple_of(where[4 + n] * 16, 16), 16), :] = part


def other_kernel(where, image1, image2, image3, held, pooling, first, out, new_scale, products, pooled):
    images = (image1, image2, image3)
    for n, image in enumerate(images):
        power_products(products, 12 * ROWS + ROWS * n, image)
        for date in range(2):
            cross_products(
                products, 2 * ROWS * (2 * n + date), image, held.at[2 + date], slice(ROWS * n, ROWS * n + ROWS)
            )
    pooled[...] = dot(products[...], pooling[...])
    sums = window_rows(pooled, 15 * ROWS)
    scale = lax.rsqrt(sums[192:240] + EPSILON)
    new_scale[...] = scale
    put(where, 0, out, first[...])
    for n in range(3):
        part = sums[64 * n : 64 * n + 64].reshape(2, 2, 16, 128)
        put(where, n + 1, out, part * scale[16 * n : 16 * n + 16])


def cross_others(where, images, held, pooling, first):
    return pl.pallas_call(
        other_kernel,
        out_shape=(jax.ShapeDtypeStruct((2, 2, 64, 128), F32), jax.ShapeDtypeStruct((48, 128), F32)),
        in_specs=[SMEM] + [VMEM] * 6,
        out_specs=(VMEM, VMEM),
        scratch_shapes=[pltpu.VMEM((15 * ROWS, A), BF16), pltpu.VMEM((15 * ROWS, 128), F32)],
        compiler_params=params(24),
        cost_estimate=cost(10**9, 9 * 10**6),
        name="cross_others",
    )(where, *images, held, pooling, first)


def own_kernel(where, order, image1, image2, image3, held, pooling, first, new_scale, scales, out, products, pooled, total):
    for n, image in enumerate((image1, image2, image3)):
        for date in range(2):
            cross_products(products, 2 * ROWS * (2 * n + date), image, held.at[date], slice(ROWS * n, ROWS * n + ROWS))
    pooled[...] = dot(products[...], pooling[...])
    sums = window_rows(pooled, 12 * ROWS)
    put(where, 0, total, first[...])
    for n in range(3):
        part = sums[64 * n : 64 * n + 64].reshape(2, 2, 16, 128)
        put(where, n + 1, total, part * new_scale[16 * n : 16 * n + 16])
    rows = pl.ds(pl.multiple_of(where[8] * 64, 64), 64)
    for n in range(2):
        slot = order[n] - where[9]
        out[n, :, rows, :] = total[slot] * scales[slot, rows, :]


def cross_own(where, order, images, held, pooling, first, new_scale, scales):
    return pl.pallas_call(
        own_kernel,
        out_shape=jax.ShapeDtypeStruct((2, 2, 128, 128), F32),
        in_specs=[SMEM] * 2 + [VMEM] * 8,
        out_specs=VMEM,
        scratch_shapes=[
            pltpu.VMEM((12 * ROWS, A), BF16),
            pltpu.VMEM((12 * ROWS, 128), F32),
            pltpu.VMEM((2, 2, 64, 128), F32),
        ],
        compiler_params=params(24),
        cost_estimate=cost(10**9, 9 * 10**6),
        name="cross_own",
    )(where, order, *images, held, pooling, first, new_scale, scales)


def final_kernel(where, order, half, received, scales, out):
    rows = pl.ds(pl.multiple_of(where[8] * 64, 64), 64)
    out[:, :, rows, :] = half[:, :, rows, :]
    rows = pl.ds(pl.multiple_of((1 - where[8]) * 64, 64), 64)
    for n in range(2):
        slot = order[n] - where[9]
        out[n, :, rows, :] = received[slot] * scales[slot, rows, :]


def assemble(where, order, half, received, scales):
    return pl.pallas_call(
        final_kernel,
        out_shape=jax.ShapeDtypeStruct((2, 2, 128, 128), F32),
        in_specs=[SMEM] * 2 + [VMEM] * 3,
        out_specs=VMEM,
        compiler_params=params(24),
        cost_estimate=cost(10**6, 10**6),
        name="assemble",
    )(where, order, half, received, scales)


def pairs(step):
    out = []
    for date in range(16):
        zh, y, core = step(date // 8, date // 2 % 4, date % 2)
        out.append((date, zh * 8 + y % 4 * 2 + core))
    return out


OTHER_CORE = pairs(lambda zh, y, core: (zh, y, 1 - core))
OTHER_Z = pairs(lambda zh, y, core: (1 - zh, y, core))
NEXT_Y = pairs(lambda zh, y, core: (zh, y + 1, core))
LAST_Y = pairs(lambda zh, y, core: (zh, y + 3, core))


def on_device(raw_echoes, range_phase, azimuth_phase, archive, date_order):
    date = lax.axis_index("date")
    zh, y, core = date // 8, date // 2 % 4, date % 2
    block = (y + 2 * zh) % 4
    blocks = jnp.stack([block, (block + 2) % 4, (block + 3) % 4, (block + 1) % 4])
    where = jnp.concatenate([core * 4 + blocks, blocks, jnp.stack([core, date * 2])]).astype(jnp.int32)

    messages = compress_range(raw_echoes, range_phase)
    messages, azimuth_phase, archive = lax.optimization_barrier((messages, azimuth_phase, archive))
    lines = lax.all_to_all(messages, ALL, 0, 0, tiled=True)
    other_archive = lax.ppermute(archive, "date", OTHER_CORE)
    image = focus_columns(lines, *prepare(azimuth_phase, where))
    pooling = jnp.asarray(pooling_table())
    images = [lax.ppermute(image, "date", perm) for perm in (OTHER_Z, NEXT_Y, LAST_Y)]
    scales = old_scales(archive, pooling)
    own_first, other_first, held, pooling = cross_first(where, image, archive, other_archive, pooling)
    other_first, scales = lax.optimization_barrier((other_first, scales))
    others, new_scale = cross_others(where, images, held, pooling, other_first)
    received = lax.ppermute(others, "date", OTHER_CORE)
    half = cross_own(where, date_order, images, held, pooling, own_first, new_scale, scales)
    return assemble(where, date_order, half, received, scales)


def solution(mesh):
    return jax.shard_map(
        on_device,
        mesh=mesh,
        in_specs=(P(None, ALL, None), P(), P("pixel", None), P("date", None, "pixel", None), P("date")),
        out_specs=P("date", None, "pixel", None),
        check_vma=False,
    )
```

```python
from functools import partial
import math

import jax
import jax.numpy as jnp
import numpy as np
from jax import lax
from jax.experimental import pallas as pl
from jax.experimental.pallas import tpu as pltpu
from jax.sharding import PartitionSpec as P

F32 = jnp.float32
BF16 = jnp.bfloat16
EPSILON = 1e-06
R = 4096
A = 2048
ROWS = 64
LINES = 16
ALL = ("pixel", "date")
VMEM = pl.BlockSpec(memory_space=pltpu.VMEM)
HBM = pl.BlockSpec(memory_space=pltpu.HBM)


def cmul(a, b):
    return (a[0] * b[0] - a[1] * b[1], a[0] * b[1] + a[1] * b[0])


def turned(value, k, n, sign):
    if k == 0:
        return value
    re, im = value
    if 8 * k == n:
        return ((re - im) * math.sqrt(0.5), (im + re) * math.sqrt(0.5)) if sign > 0 else (
            (re + im) * math.sqrt(0.5),
            (im - re) * math.sqrt(0.5),
        )
    if 8 * k == 3 * n:
        return ((re + im) * -math.sqrt(0.5), (re - im) * math.sqrt(0.5)) if sign > 0 else (
            (im - re) * math.sqrt(0.5),
            (re + im) * -math.sqrt(0.5),
        )
    angle = sign * 2.0 * math.pi * k / n
    return cmul(value, (math.cos(angle), math.sin(angle)))


def fft(values, sign):
    n = len(values)
    if n == 1:
        return values
    even, odd = fft(values[0::2], sign), fft(values[1::2], sign)
    low, high = [], []
    for k in range(n // 2):
        er, ei = even[k]
        if 4 * k == n:
            tr, ti = odd[k]
            plus, minus = (er - ti, ei + tr), (er + ti, ei - tr)
            low.append(plus if sign > 0 else minus)
            high.append(minus if sign > 0 else plus)
        else:
            tr, ti = turned(odd[k], k, n, sign)
            low.append((er + tr, ei + ti))
            high.append((er - tr, ei - ti))
    return low + high


def split(table):
    table = np.asarray(table, np.float32)
    high = table.astype(BF16)
    low = (table - high.astype(np.float32)).astype(BF16)
    return high, low


def real_form(angle, sign):
    c, s = np.cos(angle), sign * np.sin(angle)
    return np.block([[c, s], [-s, c]])


def range_tables():
    t = np.arange(128)
    k1 = 4 * (t % 32) + t // 32
    angle = 2 * np.pi * np.outer(t, k1) / 128
    fwd = np.concatenate(split(real_form(angle, -1)), axis=1)
    bwd = np.concatenate(split(real_form(angle.T, 1)), axis=1)
    twist = 2 * np.pi * np.outer(np.arange(32), t) / R
    return np.stack([np.cos(twist), -np.sin(twist)]).astype(np.float32), fwd, bwd


def azimuth_tables():
    s = np.arange(128)
    fwd = np.concatenate(split(real_form(2 * np.pi * np.outer(s, s) / 128, -1).T), axis=1)
    k1 = np.arange(128)[:, None]
    i = np.arange(8)[None, :]
    twist = np.stack([np.exp(-2j * np.pi * (i + 8 * half) * k1 / A) for half in (0, 1)], axis=-1)
    twist = np.repeat(np.stack([twist.real, twist.imag]), 64, axis=-1).transpose(0, 2, 1, 3).astype(np.float32)
    odd = np.exp(-2j * np.pi * np.arange(8)[:, None] / 16 * (np.arange(128)[None, :] // 64))
    k, lam = np.meshgrid(np.arange(8), np.arange(8), indexing="ij")
    m = (lam + 16 * k).reshape(64)
    beta = np.arange(128)
    parts = [real_form(2 * np.pi * np.outer(m + 8 * par, beta) / 128, 1) for par in (0, 1)]
    bwd = np.concatenate(split(np.concatenate(parts, axis=0)), axis=1)
    last = 2 * np.pi * np.outer(np.arange(16), beta) / A
    rows = np.concatenate([np.exp(1j * last), odd], axis=0)
    rows = np.stack([rows.real, rows.imag]).astype(np.float32)
    return twist, np.concatenate([fwd, bwd], axis=0), rows


def pooling_table():
    return (np.arange(A)[:, None] // 16 == np.arange(128)[None, :]).astype(BF16)


def dot(a, b):
    return jnp.dot(a, b, preferred_element_type=F32)


def halves(x):
    high = x.astype(BF16)
    return high, (x - high.astype(F32)).astype(BF16)


def dot_split(x, table):
    high, low = halves(x)
    n = table.shape[1] // 2
    return dot(high, table[:, :n]) + dot(low, table[:, :n]) + dot(high, table[:, n:])


def params(mib):
    return pltpu.CompilerParams(vmem_limit_bytes=mib * 2**20)


def cost(flops, moved, transcendentals=0):
    return pl.CostEstimate(flops=flops, bytes_accessed=moved, transcendentals=transcendentals)


def in_hbm(*arrays):
    return [pltpu.with_memory_space_constraint(x, pltpu.HBM) for x in arrays]


def in_vmem(*arrays):
    return [pltpu.with_memory_space_constraint(x, pltpu.VMEM) for x in arrays]


def fetch(sources, targets, sems):
    copies = [
        pltpu.make_async_copy(source, target, sems.at[n]) for n, (source, target) in enumerate(zip(sources, targets))
    ]
    for copy in copies:
        copy.start()
    return copies


def place():
    date = lax.axis_index("date")
    zh, y, core = lax.shift_right_logical(date, 3), lax.shift_right_logical(date, 1) & 3, date & 1
    block = (y + 2 * zh) & 3
    return core, (block, (block + 2) & 3, (block + 3) & 3, (block + 1) & 3)


def archive_rows(n):
    core, blocks = place()
    return pl.ds(pl.multiple_of((4 * core + blocks[n]) * ROWS, ROWS), ROWS)


def range_kernel(raw_hbm, phase_hbm, twist_hbm, fwd_hbm, bwd_hbm, out, raw, phase, twist, fwd, bwd, a, b, sems):
    copies = fetch(
        (phase_hbm, raw_hbm, twist_hbm, fwd_hbm, bwd_hbm), (phase, raw, twist, fwd, bwd), sems
    )
    copies[0].wait()
    angle = phase[...]
    angle = jnp.concatenate(
        [angle] + [pltpu.roll(angle, 128 - 32 * g, 1) for g in range(1, 4)], axis=0
    ).T[0:32]
    cosine, sine = jnp.cos(angle) * (1.0 / R), jnp.sin(angle) * (1.0 / R)
    copies[1].wait()
    copies[2].wait()
    values = [
        (raw[0, :, 128 * q : 128 * q + 128].astype(F32), raw[1, :, 128 * q : 128 * q + 128].astype(F32))
        for q in range(32)
    ]
    for k0, value in enumerate(fft(values, -1)):
        re, im = cmul(value, (twist[0, k0 : k0 + 1, :], twist[1, k0 : k0 + 1, :]))
        a[16 * k0 : 16 * k0 + 16, 0:128] = re
        a[16 * k0 : 16 * k0 + 16, 128:256] = im
    copies[3].wait()
    b[...] = dot_split(a[...], fwd)
    for k0 in range(32):
        rows = slice(16 * k0, 16 * k0 + 16)
        re, im = cmul((b[rows, 0:128], b[rows, 128:256]), (cosine[k0 : k0 + 1], sine[k0 : k0 + 1]))
        a[rows, 0:128] = re
        a[rows, 128:256] = im
    copies[4].wait()
    b[...] = dot_split(a[...], bwd)
    values = []
    for k0 in range(32):
        rows = slice(16 * k0, 16 * k0 + 16)
        values.append(
            cmul((b[rows, 0:128], b[rows, 128:256]), (twist[0, k0 : k0 + 1, :], -twist[1, k0 : k0 + 1, :]))
        )
    left = lax.broadcasted_iota(jnp.int32, (8, 128), 1) < 64
    for q, value in enumerate(fft(values, 1)):
        for half in range(2):
            parts = []
            for part in value:
                low, high = part[0:8], part[8:16]
                if half == 0:
                    parts.append(jnp.where(left, low, pltpu.roll(high, 64, 1)))
                else:
                    parts.append(jnp.where(left, pltpu.roll(low, 64, 1), high))
            message = jnp.concatenate(parts, axis=0).astype(BF16)
            pixel, core, block = q // 4, (q // 2) % 2, 2 * (q % 2) + half
            for zh in range(2):
                y = (block + 2 * zh) % 4
                out[pixel * 16 + zh * 8 + y * 2 + core] = message


def compress_range(raw, phase):
    twist, fwd, bwd = range_tables()
    return pl.pallas_call(
        range_kernel,
        out_shape=jax.ShapeDtypeStruct((128, 16, 128), BF16),
        in_specs=[HBM] * 5,
        out_specs=VMEM,
        scratch_shapes=[
            pltpu.VMEM((2, 16, R), BF16),
            pltpu.VMEM((32, 128), F32),
            pltpu.VMEM((2, 32, 128), F32),
            pltpu.VMEM((256, 512), BF16),
            pltpu.VMEM((256, 512), BF16),
            pltpu.VMEM((512, 256), F32),
            pltpu.VMEM((512, 256), F32),
            pltpu.SemaphoreType.DMA((5,)),
        ],
        compiler_params=params(24),
        cost_estimate=cost(4 * 10**8, 2 * 10**6, 8192),
        name="compress_range",
    )(*in_hbm(raw, phase.reshape(32, 128), *map(jnp.asarray, (twist, fwd, bwd))))


def prepare_kernel(angle_hbm, twist_hbm, mats_hbm, last_hbm, factors, mats, last, angle, sems):
    rows = archive_rows(0)
    copies = fetch(
        (angle_hbm.at[rows], twist_hbm, mats_hbm, last_hbm),
        (angle, factors.at[2:4], mats, last),
        sems,
    )
    copies[0].wait()
    for k in range(8):
        block = jnp.concatenate(
            [angle[:, 256 * k : 256 * k + 128], angle[:, 256 * k + 128 : 256 * k + 256]], axis=0
        )
        turned_block = block.astype(F32).T
        factors[0, k] = jnp.cos(turned_block) * (1.0 / A)
        factors[1, k] = jnp.sin(turned_block) * (1.0 / A)
    for copy in copies[1:]:
        copy.wait()


def prepare(azimuth_phase):
    tables = azimuth_tables()
    return pl.pallas_call(
        prepare_kernel,
        out_shape=(pltpu.VMEM((4, 8, 128, 128), F32), *(pltpu.VMEM(t.shape, t.dtype) for t in tables[1:])),
        in_specs=[HBM] * 4,
        out_specs=(VMEM,) * 3,
        scratch_shapes=[pltpu.VMEM((ROWS, A), BF16), pltpu.SemaphoreType.DMA((4,))],
        compiler_params=params(24),
        cost_estimate=cost(10**7, 8 * 10**6, 262144),
        name="prepare",
    )(*in_hbm(azimuth_phase, *map(jnp.asarray, tables)))


def focus_kernel(lines, factors, mats, last, out, wide, packed, spec, filtered, turned_rows, parts):
    wide[...] = lines[...].reshape(2048, 128).astype(F32)
    for j in range(16):
        ri, i = j // 8, j % 8
        packed[128 * ri : 128 * ri + 128, 128 * i : 128 * i + 128] = wide[pl.ds(j, 128, stride=16), :].astype(BF16)
    spec[...] = dot(mats[0:256, 0:256], packed[...]) + dot(mats[0:256, 256:512], packed[...])

    sign = jnp.where(lax.broadcasted_iota(jnp.int32, (8, 128), 1) < 64, 1.0, -1.0)

    def tile(step, carry):
        rows = pl.ds(pl.multiple_of(step * 8, 8), 8)
        below = pl.ds(pl.multiple_of(step * 8 + 128, 8), 8)
        values = []
        for i in range(8):
            lanes = slice(128 * i, 128 * i + 128)
            value = cmul((spec[rows, lanes], spec[below, lanes]), (factors[2, i, rows, :], factors[3, i, rows, :]))
            value = tuple(pltpu.roll(part, 64, 1) + part * sign for part in value)
            if i:
                value = cmul(value, (last[0, 16 + i : 17 + i, :], last[1, 16 + i : 17 + i, :]))
            values.append(value)
        for k, value in enumerate(fft(values, -1)):
            re, im = cmul(value, (factors[0, k, rows, :], factors[1, k, rows, :]))
            filtered[0, k, rows, :] = re
            filtered[1, k, rows, :] = im
        return carry

    lax.fori_loop(0, 16, tile, 0, unroll=4)

    for kappa in range(16):
        block = jnp.concatenate(
            [filtered[ri, k, pl.ds(kappa, 8, stride=16), :] for ri in range(2) for k in range(8)], axis=0
        )
        for n, part in enumerate(halves(block.T)):
            turned_rows[64 * kappa : 64 * kappa + 64, 256 * n : 256 * n + 128] = part[0:64]
            turned_rows[64 * kappa : 64 * kappa + 64, 256 * n + 128 : 256 * n + 256] = part[64:128]
    bwd_high, bwd_low = mats[256:512, 0:256], mats[256:512, 256:512]
    parts[...] = (
        dot(turned_rows[:, 0:256], bwd_high) + dot(turned_rows[:, 256:512], bwd_high) + dot(turned_rows[:, 0:256], bwd_low)
    )

    for step in range(4):
        rows = slice(16 * step, 16 * step + 16)
        values = []
        for kappa in range(16):
            here = slice(16 * step + 64 * kappa, 16 * step + 64 * kappa + 16)
            values.append(
                cmul(
                    (parts[here, 0:128], parts[here, 128:256]),
                    (last[0, kappa : kappa + 1, :], last[1, kappa : kappa + 1, :]),
                )
            )
        for alpha, (re, im) in enumerate(fft(values, 1)):
            lanes = slice(128 * alpha, 128 * alpha + 128)
            out[0, rows, lanes] = re.astype(BF16)
            out[1, rows, lanes] = im.astype(BF16)


def focus_columns(lines, factors, mats, last):
    return pl.pallas_call(
        focus_kernel,
        out_shape=jax.ShapeDtypeStruct((2, ROWS, A), BF16),
        in_specs=[VMEM] * 4,
        out_specs=VMEM,
        scratch_shapes=[
            pltpu.VMEM((2048, 128), F32),
            pltpu.VMEM((256, 1024), BF16),
            pltpu.VMEM((256, 1024), F32),
            pltpu.VMEM((2, 8, 128, 128), F32),
            pltpu.VMEM((1024, 512), BF16),
            pltpu.VMEM((1024, 256), F32),
        ],
        compiler_params=params(24),
        cost_estimate=cost(10**9, 4 * 10**6),
        name="focus_columns",
    )(lines, factors, mats, last)


def window_rows(pooled, row_count):
    return sum(pooled[pl.ds(j, row_count // 4, stride=4), :] for j in range(4)) * (1.0 / 64)


def inverse_root(power):
    return lax.rsqrt(power + EPSILON)


CHUNKS = [slice(256 * n, 256 * n + 256) for n in range(A // 256)]


def cross_products(products, row, image, old, old_rows):
    for lanes in CHUNKS:
        new_re, new_im = image[0, :, lanes], image[1, :, lanes]
        old_re, old_im = old[0, old_rows, lanes], old[1, old_rows, lanes]
        products[row : row + ROWS, lanes] = new_re * old_re + new_im * old_im
        products[row + ROWS : row + 2 * ROWS, lanes] = new_im * old_re - new_re * old_im


def power_products(products, row, image, rows):
    for lanes in CHUNKS:
        re, im = image[0, rows, lanes], image[1, rows, lanes]
        products[row : row + ROWS, lanes] = re * re + im * im


ALL_ROWS = slice(0, ROWS)


def block_rows(n):
    return slice(ROWS * n, ROWS * n + ROWS)


def pool(products, pooling, pooled, count):
    pooled[0 : count * ROWS, :] = dot(products[0 : count * ROWS, :], pooling[...])
    return window_rows(pooled.at[0 : count * ROWS], count * ROWS).reshape(count, 16, 128)


def scratch(count):
    return [pltpu.VMEM((count * ROWS, A), BF16), pltpu.VMEM((count * ROWS, 128), F32)]


def first_kernel(
    image, own, other, pooling_hbm, first, held, old_scales, pooling, here, products, pooled, sems
):
    copies = []
    for n in range(4):
        rows = archive_rows(n)
        for m, source in enumerate((own, other)):
            if n == 0:
                target = here.at[2 * m : 2 * m + 2]
            else:
                target = held.at[2 * m : 2 * m + 2, :, block_rows(n - 1)]
            copies.append(pltpu.make_async_copy(source.at[:, :, rows], target, sems.at[2 * n + m]))
            copies[-1].start()
    copies.append(pltpu.make_async_copy(pooling_hbm, pooling, sems.at[8]))
    copies[-1].start()
    power_products(products, 12 * ROWS, image, ALL_ROWS)
    copies[0].wait()
    copies[1].wait()
    for date in range(4):
        cross_products(products, 2 * date * ROWS, image, here.at[date], ALL_ROWS)
        power_products(products, (8 + date) * ROWS, here.at[date], ALL_ROWS)
    copies[8].wait()
    sums = pool(products, pooling, pooled, 13)
    new = inverse_root(sums[12])
    for date in range(4):
        scale = new * inverse_root(sums[8 + date])
        for part in range(2):
            first[date, part] = sums[2 * date + part] * scale
    for n in range(1, 4):
        copies[2 * n].wait()
        copies[2 * n + 1].wait()
        for date in range(4):
            power_products(products, date * ROWS, held.at[date], block_rows(n - 1))
        old_scales[n - 1] = inverse_root(pool(products, pooling, pooled, 4))


def cross_first(image, own, other, pooling):
    return pl.pallas_call(
        first_kernel,
        out_shape=(
            jax.ShapeDtypeStruct((4, 2, 16, 128), F32),
            pltpu.VMEM((4, 2, 3 * ROWS, A), BF16),
            jax.ShapeDtypeStruct((3, 4, 16, 128), F32),
            pltpu.VMEM((A, 128), BF16),
        ),
        in_specs=[VMEM, HBM, HBM, HBM],
        out_specs=(VMEM,) * 4,
        scratch_shapes=[pltpu.VMEM((4, 2, ROWS, A), BF16), *scratch(13), pltpu.SemaphoreType.DMA((9,))],
        compiler_params=params(24),
        cost_estimate=cost(10**9, 8 * 10**6),
        name="cross_first",
    )(image, *in_hbm(own, other, pooling))


def block_kernel(n, image, held, old_scales, pooling, out, products, pooled):
    for date in range(4):
        cross_products(products, 2 * date * ROWS, image, held.at[date], block_rows(n))
    power_products(products, 8 * ROWS, image, ALL_ROWS)
    sums = pool(products, pooling, pooled, 9)
    new = inverse_root(sums[8])
    for date in range(4):
        scale = new * old_scales[n, date]
        for part in range(2):
            out[date, part] = sums[2 * date + part] * scale


def cross_block(n, image, held, old_scales, pooling):
    return pl.pallas_call(
        partial(block_kernel, n),
        out_shape=jax.ShapeDtypeStruct((4, 2, 16, 128), F32),
        in_specs=[VMEM] * 4,
        out_specs=VMEM,
        scratch_shapes=scratch(9),
        compiler_params=params(24),
        cost_estimate=cost(10**8, 4 * 10**6),
        name="cross_block",
    )(image, held, old_scales, pooling)


def put(n, target, parts):
    target[:, :, pl.ds(pl.multiple_of(place()[1][n] * 16, 16), 16), :] = parts


def other_kernel(image, held, old_scales, pooling, part0, part1, part2, out, new_scale, products, pooled):
    for date in range(2):
        cross_products(products, 2 * date * ROWS, image, held.at[2 + date], block_rows(2))
    power_products(products, 4 * ROWS, image, ALL_ROWS)
    for n, part in enumerate((part0, part1, part2)):
        put(n, out, part[2:4])
    sums = pool(products, pooling, pooled, 5)
    new = inverse_root(sums[4])
    new_scale[...] = new
    put(3, out, sums[0:4].reshape(2, 2, 16, 128) * (new * old_scales[2, 2:4])[:, None])


def cross_others(image, held, old_scales, pooling, parts):
    return pl.pallas_call(
        other_kernel,
        out_shape=(jax.ShapeDtypeStruct((2, 2, 64, 128), F32), jax.ShapeDtypeStruct((16, 128), F32)),
        in_specs=[VMEM] * 7,
        out_specs=(VMEM, VMEM),
        scratch_shapes=scratch(5),
        compiler_params=params(24),
        cost_estimate=cost(10**8, 4 * 10**6),
        name="cross_others",
    )(image, held, old_scales, pooling, *parts)


def own_kernel(image, held, old_scales, pooling, part0, part1, part2, new_scale, out, products, pooled):
    for date in range(2):
        cross_products(products, 2 * date * ROWS, image, held.at[date], block_rows(2))
    for n, part in enumerate((part0, part1, part2)):
        put(n, out, part[0:2])
    sums = pool(products, pooling, pooled, 4)
    put(3, out, sums.reshape(2, 2, 16, 128) * (new_scale[...] * old_scales[2, 0:2])[:, None])


def cross_own(image, held, old_scales, pooling, parts, new_scale):
    return pl.pallas_call(
        own_kernel,
        out_shape=jax.ShapeDtypeStruct((2, 2, 64, 128), F32),
        in_specs=[VMEM] * 8,
        out_specs=VMEM,
        scratch_shapes=scratch(4),
        compiler_params=params(24),
        cost_estimate=cost(10**8, 4 * 10**6),
        name="cross_own",
    )(image, held, old_scales, pooling, *parts, new_scale)


def final_kernel(order, mine, received, out):
    core, _ = place()
    odd_first = order[...] & 1 == 1
    for half, source in ((core, mine), (1 - core, received)):
        rows = pl.ds(pl.multiple_of(half * 64, 64), 64)
        for part in range(2):
            even, odd = source[0, part], source[1, part]
            out[0, part, rows, :] = jnp.where(odd_first, odd, even)
            out[1, part, rows, :] = jnp.where(odd_first, even, odd)


def assemble(date_order, mine, received):
    return pl.pallas_call(
        final_kernel,
        out_shape=jax.ShapeDtypeStruct((2, 2, 128, 128), F32),
        in_specs=[VMEM] * 3,
        out_specs=VMEM,
        compiler_params=params(24),
        cost_estimate=cost(10**6, 10**6),
        name="assemble",
    )(jnp.broadcast_to(date_order[0], (1, 128)), mine, received)


def pairs(step):
    out = []
    for date in range(16):
        zh, y, core = step(date // 8, date // 2 % 4, date % 2)
        out.append((date, zh * 8 + y % 4 * 2 + core))
    return out


OTHER_CORE = pairs(lambda zh, y, core: (zh, y, 1 - core))
OTHER_Z = pairs(lambda zh, y, core: (1 - zh, y, core))
NEXT_Y = pairs(lambda zh, y, core: (zh, y + 1, core))
LAST_Y = pairs(lambda zh, y, core: (zh, y + 3, core))


def on_device(raw_echoes, range_phase, azimuth_phase, archive, date_order):
    messages = compress_range(raw_echoes, range_phase)
    messages, azimuth_phase, archive = lax.optimization_barrier((messages, azimuth_phase, archive))
    lines = lax.all_to_all(messages, ALL, 0, 0, tiled=True)
    other_archive = lax.ppermute(archive, "date", OTHER_CORE)
    image = focus_columns(lines, *prepare(azimuth_phase))
    images = [lax.ppermute(image, "date", perm) for perm in (OTHER_Z, NEXT_Y, LAST_Y)]
    first, *kept = cross_first(image, archive, other_archive, jnp.asarray(pooling_table()))
    parts = [first] + [cross_block(n, images[n], *kept) for n in range(2)]
    others, new_scale = cross_others(images[2], *kept, parts)
    received = lax.ppermute(others, "date", OTHER_CORE)
    mine = cross_own(images[2], *kept, parts, new_scale)
    return assemble(date_order, mine, received)


def solution(mesh):
    return jax.shard_map(
        on_device,
        mesh=mesh,
        in_specs=(P(None, ALL, None), P(), P("pixel", None), P("date", None, "pixel", None), P("date")),
        out_specs=P("date", None, "pixel", None),
        check_vma=False,
    )
```

```python
from functools import partial
import math

import jax
import jax.numpy as jnp
import numpy as np
from jax import lax
from jax.experimental import pallas as pl
from jax.experimental.pallas import tpu as pltpu
from jax.sharding import PartitionSpec as P

F32 = jnp.float32
BF16 = jnp.bfloat16
EPSILON = 1e-06
R = 4096
A = 2048
ROWS = 64
LINES = 16
ALL = ("pixel", "date")
VMEM = pl.BlockSpec(memory_space=pltpu.VMEM)
HBM = pl.BlockSpec(memory_space=pltpu.HBM)


def cmul(a, b):
    return (a[0] * b[0] - a[1] * b[1], a[0] * b[1] + a[1] * b[0])


def turned(value, k, n, sign):
    if k == 0:
        return value
    re, im = value
    if 8 * k == n:
        return ((re - im) * math.sqrt(0.5), (im + re) * math.sqrt(0.5)) if sign > 0 else (
            (re + im) * math.sqrt(0.5),
            (im - re) * math.sqrt(0.5),
        )
    if 8 * k == 3 * n:
        return ((re + im) * -math.sqrt(0.5), (re - im) * math.sqrt(0.5)) if sign > 0 else (
            (im - re) * math.sqrt(0.5),
            (re + im) * -math.sqrt(0.5),
        )
    angle = sign * 2.0 * math.pi * k / n
    return cmul(value, (math.cos(angle), math.sin(angle)))


def fft(values, sign):
    n = len(values)
    if n == 1:
        return values
    even, odd = fft(values[0::2], sign), fft(values[1::2], sign)
    low, high = [], []
    for k in range(n // 2):
        er, ei = even[k]
        if 4 * k == n:
            tr, ti = odd[k]
            plus, minus = (er - ti, ei + tr), (er + ti, ei - tr)
            low.append(plus if sign > 0 else minus)
            high.append(minus if sign > 0 else plus)
        else:
            tr, ti = turned(odd[k], k, n, sign)
            low.append((er + tr, ei + ti))
            high.append((er - tr, ei - ti))
    return low + high


def split(table):
    table = np.asarray(table, np.float32)
    high = table.astype(BF16)
    low = (table - high.astype(np.float32)).astype(BF16)
    return high, low


def real_form(angle, sign):
    c, s = np.cos(angle), sign * np.sin(angle)
    return np.block([[c, s], [-s, c]])


def range_tables():
    t = np.arange(128)
    k1 = 4 * (t % 32) + t // 32
    angle = 2 * np.pi * np.outer(t, k1) / 128
    fwd, bwd = (
        np.concatenate([high, high, low], axis=0)
        for high, low in (split(real_form(angle, -1)), split(real_form(angle.T, 1)))
    )
    twist = 2 * np.pi * np.outer(np.arange(32), t) / R
    return np.stack([np.cos(twist), -np.sin(twist)]).astype(np.float32), fwd, bwd


def azimuth_tables():
    s = np.arange(128)
    fwd = np.concatenate(split(real_form(2 * np.pi * np.outer(s, s) / 128, -1).T), axis=1)
    k1 = np.arange(128)[:, None]
    i = np.arange(8)[None, :]
    twist = np.stack([np.exp(-2j * np.pi * (i + 8 * half) * k1 / A) for half in (0, 1)], axis=-1)
    twist = np.repeat(np.stack([twist.real, twist.imag]), 64, axis=-1).transpose(0, 2, 1, 3).astype(np.float32)
    odd = np.exp(-2j * np.pi * np.arange(8)[:, None] / 16 * (np.arange(128)[None, :] // 64))
    k, lam = np.meshgrid(np.arange(8), np.arange(8), indexing="ij")
    m = (lam + 16 * k).reshape(64)
    beta = np.arange(128)
    parts = [real_form(2 * np.pi * np.outer(m + 8 * par, beta) / 128, 1) for par in (0, 1)]
    bwd = np.concatenate(split(np.concatenate(parts, axis=0)), axis=1)
    last = 2 * np.pi * np.outer(np.arange(16), beta) / A
    rows = np.concatenate([np.exp(1j * last), odd], axis=0)
    rows = np.stack([rows.real, rows.imag]).astype(np.float32)
    return twist, np.concatenate([fwd, bwd], axis=0), rows


def pooling_table():
    return (np.arange(A)[:, None] // 16 == np.arange(128)[None, :]).astype(BF16)


def dot(a, b):
    return jnp.dot(a, b, preferred_element_type=F32)


def halves(x):
    high = x.astype(BF16)
    return high, (x - high.astype(F32)).astype(BF16)


def keep(target, rows, re, im):
    (re_high, re_low), (im_high, im_low) = halves(re), halves(im)
    target[rows, 0:128] = re_high
    target[rows, 128:256] = im_high
    target[rows, 256:384] = re_low
    target[rows, 384:512] = im_low


def dot_split(x, table):
    return dot(x[...], table[0:512]) + dot(x[:, 0:256], table[512:768])


def params(mib):
    return pltpu.CompilerParams(vmem_limit_bytes=mib * 2**20)


def cost(flops, moved, transcendentals=0):
    return pl.CostEstimate(flops=flops, bytes_accessed=moved, transcendentals=transcendentals)


def in_hbm(*arrays):
    return [pltpu.with_memory_space_constraint(x, pltpu.HBM) for x in arrays]


def in_vmem(*arrays):
    return [pltpu.with_memory_space_constraint(x, pltpu.VMEM) for x in arrays]


def fetch(sources, targets, sems):
    copies = [
        pltpu.make_async_copy(source, target, sems.at[n]) for n, (source, target) in enumerate(zip(sources, targets))
    ]
    for copy in copies:
        copy.start()
    return copies


def place():
    date = lax.axis_index("date")
    zh, y, core = lax.shift_right_logical(date, 3), lax.shift_right_logical(date, 1) & 3, date & 1
    block = (y + 2 * zh) & 3
    return core, (block, (block + 3) & 3, (block + 2) & 3, (block + 1) & 3)


def archive_rows(n):
    core, blocks = place()
    return pl.ds(pl.multiple_of((4 * core + blocks[n]) * ROWS, ROWS), ROWS)


def range_kernel(raw_hbm, phase_hbm, twist_hbm, fwd_hbm, bwd_hbm, out, raw, phase, twist, fwd, bwd, a, b, sems):
    copies = fetch(
        (phase_hbm, raw_hbm, twist_hbm, fwd_hbm, bwd_hbm), (phase, raw, twist, fwd, bwd), sems
    )
    copies[0].wait()
    angle = phase[...]
    angle = jnp.concatenate(
        [angle] + [pltpu.roll(angle, 128 - 32 * g, 1) for g in range(1, 4)], axis=0
    ).T[0:32]
    cosine, sine = jnp.cos(angle) * (1.0 / R), jnp.sin(angle) * (1.0 / R)
    copies[1].wait()
    copies[2].wait()
    values = [
        (raw[0, :, 128 * q : 128 * q + 128].astype(F32), raw[1, :, 128 * q : 128 * q + 128].astype(F32))
        for q in range(32)
    ]
    for k0, value in enumerate(fft(values, -1)):
        re, im = cmul(value, (twist[0, k0 : k0 + 1, :], twist[1, k0 : k0 + 1, :]))
        keep(a, slice(16 * k0, 16 * k0 + 16), re, im)
    copies[3].wait()
    b[...] = dot_split(a, fwd)
    for k0 in range(32):
        rows = slice(16 * k0, 16 * k0 + 16)
        re, im = cmul((b[rows, 0:128], b[rows, 128:256]), (cosine[k0 : k0 + 1], sine[k0 : k0 + 1]))
        keep(a, rows, re, im)
    copies[4].wait()
    b[...] = dot_split(a, bwd)
    values = []
    for k0 in range(32):
        rows = slice(16 * k0, 16 * k0 + 16)
        values.append(
            cmul((b[rows, 0:128], b[rows, 128:256]), (twist[0, k0 : k0 + 1, :], -twist[1, k0 : k0 + 1, :]))
        )
    left = lax.broadcasted_iota(jnp.int32, (8, 128), 1) < 64
    for q, value in enumerate(fft(values, 1)):
        pixel, core = q // 4, (q // 2) % 2
        for half in range(2):
            parts = []
            for part in value:
                low, high = part[0:8], part[8:16]
                if half == 0:
                    parts.append(jnp.where(left, low, pltpu.roll(high, 64, 1)))
                else:
                    parts.append(jnp.where(left, pltpu.roll(low, 64, 1), high))
            message = jnp.concatenate(parts, axis=0).astype(BF16)
            block = 2 * (q % 2) + half
            for zh in range(2):
                y = (block + 2 * zh) % 4
                out[pixel * 16 + zh * 8 + y * 2 + core] = message


def compress_range(raw, phase):
    twist, fwd, bwd = range_tables()
    return pl.pallas_call(
        range_kernel,
        out_shape=jax.ShapeDtypeStruct((128, 16, 128), BF16),
        in_specs=[HBM] * 5,
        out_specs=VMEM,
        scratch_shapes=[
            pltpu.VMEM((2, 16, R), BF16),
            pltpu.VMEM((32, 128), F32),
            pltpu.VMEM((2, 32, 128), F32),
            pltpu.VMEM((768, 256), BF16),
            pltpu.VMEM((768, 256), BF16),
            pltpu.VMEM((512, 512), BF16),
            pltpu.VMEM((512, 256), F32),
            pltpu.SemaphoreType.DMA((5,)),
        ],
        compiler_params=params(24),
        cost_estimate=cost(4 * 10**8, 2 * 10**6, 8192),
        name="compress_range",
    )(*in_hbm(raw, phase.reshape(32, 128), *map(jnp.asarray, (twist, fwd, bwd))))


def prepare_kernel(angle_hbm, twist_hbm, mats_hbm, last_hbm, factors, mats, last, angle, sems):
    rows = archive_rows(0)
    copies = fetch(
        (angle_hbm.at[rows], twist_hbm, mats_hbm, last_hbm),
        (angle, factors.at[2:4], mats, last),
        sems,
    )
    copies[0].wait()
    for k in range(8):
        block = jnp.concatenate(
            [angle[:, 256 * k : 256 * k + 128], angle[:, 256 * k + 128 : 256 * k + 256]], axis=0
        )
        turned_block = block.astype(F32).T
        factors[0, k] = jnp.cos(turned_block) * (1.0 / A)
        factors[1, k] = jnp.sin(turned_block) * (1.0 / A)
    for copy in copies[1:]:
        copy.wait()


def prepare(azimuth_phase):
    tables = azimuth_tables()
    return pl.pallas_call(
        prepare_kernel,
        out_shape=(pltpu.VMEM((4, 8, 128, 128), F32), *(pltpu.VMEM(t.shape, t.dtype) for t in tables[1:])),
        in_specs=[HBM] * 4,
        out_specs=(VMEM,) * 3,
        scratch_shapes=[pltpu.VMEM((ROWS, A), BF16), pltpu.SemaphoreType.DMA((4,))],
        compiler_params=params(24),
        cost_estimate=cost(10**7, 8 * 10**6, 262144),
        name="prepare",
    )(*in_hbm(azimuth_phase, *map(jnp.asarray, tables)))


def focus_kernel(lines, factors, mats, last, out, wide, packed, spec, filtered, turned_rows, parts):
    wide[...] = lines[...].reshape(2048, 128).astype(F32)
    for j in range(16):
        ri, i = j // 8, j % 8
        packed[128 * ri : 128 * ri + 128, 128 * i : 128 * i + 128] = wide[pl.ds(j, 128, stride=16), :].astype(BF16)
    spec[...] = dot(mats[0:256, 0:256], packed[...]) + dot(mats[0:256, 256:512], packed[...])

    sign = jnp.where(lax.broadcasted_iota(jnp.int32, (8, 128), 1) < 64, 1.0, -1.0)

    def tile(step, carry):
        rows = pl.ds(pl.multiple_of(step * 8, 8), 8)
        below = pl.ds(pl.multiple_of(step * 8 + 128, 8), 8)
        values = []
        for i in range(8):
            lanes = slice(128 * i, 128 * i + 128)
            value = cmul((spec[rows, lanes], spec[below, lanes]), (factors[2, i, rows, :], factors[3, i, rows, :]))
            value = tuple(pltpu.roll(part, 64, 1) + part * sign for part in value)
            if i:
                value = cmul(value, (last[0, 16 + i : 17 + i, :], last[1, 16 + i : 17 + i, :]))
            values.append(value)
        for k, value in enumerate(fft(values, -1)):
            re, im = cmul(value, (factors[0, k, rows, :], factors[1, k, rows, :]))
            filtered[0, k, rows, :] = re
            filtered[1, k, rows, :] = im
        return carry

    lax.fori_loop(0, 16, tile, 0, unroll=True)

    for kappa in range(16):
        block = jnp.concatenate(
            [filtered[ri, k, pl.ds(kappa, 8, stride=16), :] for ri in range(2) for k in range(8)], axis=0
        )
        for n, part in enumerate(halves(block.T)):
            turned_rows[64 * kappa : 64 * kappa + 64, 256 * n : 256 * n + 128] = part[0:64]
            turned_rows[64 * kappa : 64 * kappa + 64, 256 * n + 128 : 256 * n + 256] = part[64:128]
    bwd_high, bwd_low = mats[256:512, 0:256], mats[256:512, 256:512]
    parts[...] = (
        dot(turned_rows[:, 0:256], bwd_high) + dot(turned_rows[:, 256:512], bwd_high) + dot(turned_rows[:, 0:256], bwd_low)
    )

    for step in range(4):
        rows = slice(16 * step, 16 * step + 16)
        values = []
        for kappa in range(16):
            here = slice(16 * step + 64 * kappa, 16 * step + 64 * kappa + 16)
            values.append(
                cmul(
                    (parts[here, 0:128], parts[here, 128:256]),
                    (last[0, kappa : kappa + 1, :], last[1, kappa : kappa + 1, :]),
                )
            )
        for alpha, (re, im) in enumerate(fft(values, 1)):
            lanes = slice(128 * alpha, 128 * alpha + 128)
            out[0, rows, lanes] = re.astype(BF16)
            out[1, rows, lanes] = im.astype(BF16)


def focus_columns(lines, factors, mats, last):
    return pl.pallas_call(
        focus_kernel,
        out_shape=jax.ShapeDtypeStruct((2, ROWS, A), BF16),
        in_specs=[VMEM] * 4,
        out_specs=VMEM,
        scratch_shapes=[
            pltpu.VMEM((2048, 128), F32),
            pltpu.VMEM((256, 1024), BF16),
            pltpu.VMEM((256, 1024), F32),
            pltpu.VMEM((2, 8, 128, 128), F32),
            pltpu.VMEM((1024, 512), BF16),
            pltpu.VMEM((1024, 256), F32),
        ],
        compiler_params=params(24),
        cost_estimate=cost(10**9, 4 * 10**6),
        name="focus_columns",
    )(lines, factors, mats, last)


def window_rows(pooled, row_count):
    return sum(pooled[pl.ds(j, row_count // 4, stride=4), :] for j in range(4)) * (1.0 / 64)


def inverse_root(power):
    return lax.rsqrt(power + EPSILON)


CHUNKS = [slice(256 * n, 256 * n + 256) for n in range(A // 256)]


def cross_products(products, row, image, old, old_rows):
    for lanes in CHUNKS:
        new_re, new_im = image[0, :, lanes], image[1, :, lanes]
        old_re, old_im = old[0, old_rows, lanes], old[1, old_rows, lanes]
        products[row : row + ROWS, lanes] = new_re * old_re + new_im * old_im
        products[row + ROWS : row + 2 * ROWS, lanes] = new_im * old_re - new_re * old_im


def power_products(products, row, image, rows):
    for lanes in CHUNKS:
        re, im = image[0, rows, lanes], image[1, rows, lanes]
        products[row : row + ROWS, lanes] = re * re + im * im


ALL_ROWS = slice(0, ROWS)


def block_rows(n):
    return slice(ROWS * n, ROWS * n + ROWS)


def pool(products, pooling, pooled, count):
    pooled[0 : count * ROWS, :] = dot(products[0 : count * ROWS, :], pooling[...])
    return window_rows(pooled.at[0 : count * ROWS], count * ROWS).reshape(count, 16, 128)


def scratch(count):
    return [pltpu.VMEM((count * ROWS, A), BF16), pltpu.VMEM((count * ROWS, 128), F32)]


def first_kernel(
    image, own, other, pooling_hbm, first, held, old_scales, pooling, here, products, pooled, sems
):
    copies = []
    for n in range(4):
        rows = archive_rows(n)
        for m, source in enumerate((own, other)):
            if n == 0:
                target = here.at[2 * m : 2 * m + 2]
            else:
                target = held.at[2 * m : 2 * m + 2, :, block_rows(n - 1)]
            copies.append(pltpu.make_async_copy(source.at[:, :, rows], target, sems.at[2 * n + m]))
            copies[-1].start()
    copies.append(pltpu.make_async_copy(pooling_hbm, pooling, sems.at[8]))
    copies[-1].start()
    power_products(products, 12 * ROWS, image, ALL_ROWS)
    copies[0].wait()
    copies[1].wait()
    for date in range(4):
        cross_products(products, 2 * date * ROWS, image, here.at[date], ALL_ROWS)
        power_products(products, (8 + date) * ROWS, here.at[date], ALL_ROWS)
    copies[8].wait()
    sums = pool(products, pooling, pooled, 13)
    new = inverse_root(sums[12])
    for date in range(4):
        scale = new * inverse_root(sums[8 + date])
        for part in range(2):
            first[date, part] = sums[2 * date + part] * scale
    for n in range(1, 4):
        copies[2 * n].wait()
        copies[2 * n + 1].wait()
        for date in range(4):
            power_products(products, date * ROWS, held.at[date], block_rows(n - 1))
        old_scales[n - 1] = inverse_root(pool(products, pooling, pooled, 4))


def cross_first(image, own, other, pooling):
    return pl.pallas_call(
        first_kernel,
        out_shape=(
            jax.ShapeDtypeStruct((4, 2, 16, 128), F32),
            pltpu.VMEM((4, 2, 3 * ROWS, A), BF16),
            jax.ShapeDtypeStruct((3, 4, 16, 128), F32),
            pltpu.VMEM((A, 128), BF16),
        ),
        in_specs=[VMEM, HBM, HBM, HBM],
        out_specs=(VMEM,) * 4,
        scratch_shapes=[pltpu.VMEM((4, 2, ROWS, A), BF16), *scratch(13), pltpu.SemaphoreType.DMA((9,))],
        compiler_params=params(24),
        cost_estimate=cost(10**9, 8 * 10**6),
        name="cross_first",
    )(image, *in_hbm(own, other, pooling))


def block_kernel(n, image, held, old_scales, pooling, out, products, pooled):
    for date in range(4):
        cross_products(products, 2 * date * ROWS, image, held.at[date], block_rows(n))
    power_products(products, 8 * ROWS, image, ALL_ROWS)
    sums = pool(products, pooling, pooled, 9)
    new = inverse_root(sums[8])
    for date in range(4):
        scale = new * old_scales[n, date]
        for part in range(2):
            out[date, part] = sums[2 * date + part] * scale


def cross_block(n, image, held, old_scales, pooling):
    return pl.pallas_call(
        partial(block_kernel, n),
        out_shape=jax.ShapeDtypeStruct((4, 2, 16, 128), F32),
        in_specs=[VMEM] * 4,
        out_specs=VMEM,
        scratch_shapes=scratch(9),
        compiler_params=params(24),
        cost_estimate=cost(10**8, 4 * 10**6),
        name="cross_block",
    )(image, held, old_scales, pooling)


def put(n, target, parts):
    target[:, :, pl.ds(pl.multiple_of(place()[1][n] * 16, 16), 16), :] = parts


def other_kernel(image1, image2, held, old_scales, pooling, part0, part1, out, new_scale, products, pooled):
    for n, image in enumerate((image1, image2)):
        for date in range(2):
            cross_products(products, (4 * n + 2 * date) * ROWS, image, held.at[2 + date], block_rows(n + 1))
        power_products(products, (8 + n) * ROWS, image, ALL_ROWS)
    for n, part in enumerate((part0, part1)):
        put(n, out, part[2:4])
    sums = pool(products, pooling, pooled, 10)
    for n in range(2):
        new = inverse_root(sums[8 + n])
        new_scale[n] = new
        put(n + 2, out, sums[4 * n : 4 * n + 4].reshape(2, 2, 16, 128) * (new * old_scales[n + 1, 2:4])[:, None])


def cross_others(images, held, old_scales, pooling, parts):
    return pl.pallas_call(
        other_kernel,
        out_shape=(jax.ShapeDtypeStruct((2, 2, 64, 128), F32), jax.ShapeDtypeStruct((2, 16, 128), F32)),
        in_specs=[VMEM] * 7,
        out_specs=(VMEM, VMEM),
        scratch_shapes=scratch(10),
        compiler_params=params(24),
        cost_estimate=cost(10**8, 4 * 10**6),
        name="cross_others",
    )(*images, held, old_scales, pooling, *parts)


def own_kernel(image1, image2, held, old_scales, pooling, part0, part1, new_scale, out, products, pooled):
    for n, image in enumerate((image1, image2)):
        for date in range(2):
            cross_products(products, (4 * n + 2 * date) * ROWS, image, held.at[date], block_rows(n + 1))
    for n, part in enumerate((part0, part1)):
        put(n, out, part[0:2])
    sums = pool(products, pooling, pooled, 8)
    for n in range(2):
        scale = (new_scale[n] * old_scales[n + 1, 0:2])[:, None]
        put(n + 2, out, sums[4 * n : 4 * n + 4].reshape(2, 2, 16, 128) * scale)


def cross_own(images, held, old_scales, pooling, parts, new_scale):
    return pl.pallas_call(
        own_kernel,
        out_shape=jax.ShapeDtypeStruct((2, 2, 64, 128), F32),
        in_specs=[VMEM] * 8,
        out_specs=VMEM,
        scratch_shapes=scratch(8),
        compiler_params=params(24),
        cost_estimate=cost(10**8, 4 * 10**6),
        name="cross_own",
    )(*images, held, old_scales, pooling, *parts, new_scale)


def final_kernel(order, mine, received, out):
    core, _ = place()
    odd_first = order[...] & 1 == 1
    for half, source in ((core, mine), (1 - core, received)):
        rows = pl.ds(pl.multiple_of(half * 64, 64), 64)
        for part in range(2):
            even, odd = source[0, part], source[1, part]
            out[0, part, rows, :] = jnp.where(odd_first, odd, even)
            out[1, part, rows, :] = jnp.where(odd_first, even, odd)


def assemble(date_order, mine, received):
    return pl.pallas_call(
        final_kernel,
        out_shape=jax.ShapeDtypeStruct((2, 2, 128, 128), F32),
        in_specs=[VMEM] * 3,
        out_specs=VMEM,
        compiler_params=params(24),
        cost_estimate=cost(10**6, 10**6),
        name="assemble",
    )(jnp.broadcast_to(date_order[0], (1, 128)), mine, received)


def pairs(step):
    out = []
    for date in range(16):
        zh, y, core = step(date // 8, date // 2 % 4, date % 2)
        out.append((date, zh * 8 + y % 4 * 2 + core))
    return out


OTHER_CORE = pairs(lambda zh, y, core: (zh, y, 1 - core))
OTHER_Z = pairs(lambda zh, y, core: (1 - zh, y, core))
NEXT_Y = pairs(lambda zh, y, core: (zh, y + 1, core))
LAST_Y = pairs(lambda zh, y, core: (zh, y + 3, core))


def on_device(raw_echoes, range_phase, azimuth_phase, archive, date_order):
    messages = compress_range(raw_echoes, range_phase)
    messages, azimuth_phase, archive = lax.optimization_barrier((messages, azimuth_phase, archive))
    lines = lax.all_to_all(messages, ALL, 0, 0, tiled=True)
    other_archive = lax.ppermute(archive, "date", OTHER_CORE)
    image = focus_columns(lines, *prepare(azimuth_phase))
    images = [lax.ppermute(image, "date", perm) for perm in (NEXT_Y, OTHER_Z, LAST_Y)]
    first, *kept = cross_first(image, archive, other_archive, jnp.asarray(pooling_table()))
    parts = [first, cross_block(0, images[0], *kept)]
    others, new_scale = cross_others(images[1:], *kept, parts)
    received = lax.ppermute(others, "date", OTHER_CORE)
    mine = cross_own(images[1:], *kept, parts, new_scale)
    return assemble(date_order, mine, received)


def solution(mesh):
    return jax.shard_map(
        on_device,
        mesh=mesh,
        in_specs=(P(None, ALL, None), P(), P("pixel", None), P("date", None, "pixel", None), P("date")),
        out_specs=P("date", None, "pixel", None),
        check_vma=False,
    )
```

```python
from functools import partial
import math

import jax
import jax.numpy as jnp
import numpy as np
from jax import lax
from jax.experimental import pallas as pl
from jax.experimental.pallas import tpu as pltpu
from jax.sharding import PartitionSpec as P

F32 = jnp.float32
BF16 = jnp.bfloat16
EPSILON = 1e-06
R = 4096
A = 2048
ROWS = 64
LINES = 16
ALL = ("pixel", "date")
VMEM = pl.BlockSpec(memory_space=pltpu.VMEM)
HBM = pl.BlockSpec(memory_space=pltpu.HBM)


def cmul(a, b):
    return (a[0] * b[0] - a[1] * b[1], a[0] * b[1] + a[1] * b[0])


def turned(value, k, n, sign):
    if k == 0:
        return value
    re, im = value
    if 8 * k == n:
        return ((re - im) * math.sqrt(0.5), (im + re) * math.sqrt(0.5)) if sign > 0 else (
            (re + im) * math.sqrt(0.5),
            (im - re) * math.sqrt(0.5),
        )
    if 8 * k == 3 * n:
        return ((re + im) * -math.sqrt(0.5), (re - im) * math.sqrt(0.5)) if sign > 0 else (
            (im - re) * math.sqrt(0.5),
            (re + im) * -math.sqrt(0.5),
        )
    angle = sign * 2.0 * math.pi * k / n
    return cmul(value, (math.cos(angle), math.sin(angle)))


def fft(values, sign):
    n = len(values)
    if n == 1:
        return values
    even, odd = fft(values[0::2], sign), fft(values[1::2], sign)
    low, high = [], []
    for k in range(n // 2):
        er, ei = even[k]
        if 4 * k == n:
            tr, ti = odd[k]
            plus, minus = (er - ti, ei + tr), (er + ti, ei - tr)
            low.append(plus if sign > 0 else minus)
            high.append(minus if sign > 0 else plus)
        else:
            tr, ti = turned(odd[k], k, n, sign)
            low.append((er + tr, ei + ti))
            high.append((er - tr, ei - ti))
    return low + high


def split(table):
    table = np.asarray(table, np.float32)
    high = table.astype(BF16)
    low = (table - high.astype(np.float32)).astype(BF16)
    return high, low


def real_form(angle, sign):
    c, s = np.cos(angle), sign * np.sin(angle)
    return np.block([[c, s], [-s, c]])


def range_tables():
    t = np.arange(128)
    k1 = 4 * (t % 32) + t // 32
    angle = 2 * np.pi * np.outer(t, k1) / 128
    fwd, bwd = (
        np.concatenate([high, high, low], axis=0)
        for high, low in (split(real_form(angle, -1)), split(real_form(angle.T, 1)))
    )
    twist = 2 * np.pi * np.outer(np.arange(32), t) / R
    return np.stack([np.cos(twist), -np.sin(twist)]).astype(np.float32), fwd, bwd


def azimuth_tables():
    s = np.arange(128)
    fwd = np.concatenate(split(real_form(2 * np.pi * np.outer(s, s) / 128, -1).T), axis=1)
    k1 = np.arange(128)[:, None]
    i = np.arange(8)[None, :]
    twist = np.stack([np.exp(-2j * np.pi * (i + 8 * half) * k1 / A) for half in (0, 1)], axis=-1)
    twist = np.repeat(np.stack([twist.real, twist.imag]), 64, axis=-1).transpose(0, 2, 1, 3).astype(np.float32)
    odd = np.exp(-2j * np.pi * np.arange(8)[:, None] / 16 * (np.arange(128)[None, :] // 64))
    k, lam = np.meshgrid(np.arange(8), np.arange(8), indexing="ij")
    m = (lam + 16 * k).reshape(64)
    beta = np.arange(128)
    parts = [real_form(2 * np.pi * np.outer(m + 8 * par, beta) / 128, 1) for par in (0, 1)]
    bwd = np.concatenate(split(np.concatenate(parts, axis=0)), axis=1)
    last = 2 * np.pi * np.outer(np.arange(16), beta) / A
    rows = np.concatenate([np.exp(1j * last), odd], axis=0)
    rows = np.stack([rows.real, rows.imag]).astype(np.float32)
    return twist, np.concatenate([fwd, bwd], axis=0), rows


def pooling_table():
    return (np.arange(A)[:, None] // 16 == np.arange(128)[None, :]).astype(BF16)


def dot(a, b):
    return jnp.dot(a, b, preferred_element_type=F32)


def halves(x):
    high = x.astype(BF16)
    return high, (x - high.astype(F32)).astype(BF16)


def keep(target, rows, re, im):
    (re_high, re_low), (im_high, im_low) = halves(re), halves(im)
    target[rows, 0:128] = re_high
    target[rows, 128:256] = im_high
    target[rows, 256:384] = re_low
    target[rows, 384:512] = im_low


def dot_split(x, table):
    return dot(x[...], table[0:512]) + dot(x[:, 0:256], table[512:768])


def params(mib):
    return pltpu.CompilerParams(vmem_limit_bytes=mib * 2**20)


def cost(flops, moved, transcendentals=0):
    return pl.CostEstimate(flops=flops, bytes_accessed=moved, transcendentals=transcendentals)


def in_hbm(*arrays):
    return [pltpu.with_memory_space_constraint(x, pltpu.HBM) for x in arrays]


def in_vmem(*arrays):
    return [pltpu.with_memory_space_constraint(x, pltpu.VMEM) for x in arrays]


def fetch(sources, targets, sems):
    copies = [
        pltpu.make_async_copy(source, target, sems.at[n]) for n, (source, target) in enumerate(zip(sources, targets))
    ]
    for copy in copies:
        copy.start()
    return copies


def place():
    date = lax.axis_index("date")
    zh, y, core = lax.shift_right_logical(date, 3), lax.shift_right_logical(date, 1) & 3, date & 1
    block = (y + 2 * zh) & 3
    return core, (block, (block + 3 - 2 * core) & 3, (block + 2) & 3, (block + 1 + 2 * core) & 3)


def archive_rows(n):
    core, blocks = place()
    return pl.ds(pl.multiple_of((4 * core + blocks[n]) * ROWS, ROWS), ROWS)


def range_kernel(raw_hbm, phase_hbm, twist_hbm, fwd_hbm, bwd_hbm, out, raw, phase, twist, fwd, bwd, a, b, sems):
    copies = fetch(
        (phase_hbm, raw_hbm, twist_hbm, fwd_hbm, bwd_hbm), (phase, raw, twist, fwd, bwd), sems
    )
    copies[0].wait()
    angle = phase[...]
    angle = jnp.concatenate(
        [angle] + [pltpu.roll(angle, 128 - 32 * g, 1) for g in range(1, 4)], axis=0
    ).T[0:32]
    cosine, sine = jnp.cos(angle) * (1.0 / R), jnp.sin(angle) * (1.0 / R)
    copies[1].wait()
    copies[2].wait()
    values = [
        (raw[0, :, 128 * q : 128 * q + 128].astype(F32), raw[1, :, 128 * q : 128 * q + 128].astype(F32))
        for q in range(32)
    ]
    for k0, value in enumerate(fft(values, -1)):
        re, im = cmul(value, (twist[0, k0 : k0 + 1, :], twist[1, k0 : k0 + 1, :]))
        keep(a, slice(16 * k0, 16 * k0 + 16), re, im)
    copies[3].wait()
    b[...] = dot_split(a, fwd)
    for k0 in range(32):
        rows = slice(16 * k0, 16 * k0 + 16)
        re, im = cmul((b[rows, 0:128], b[rows, 128:256]), (cosine[k0 : k0 + 1], sine[k0 : k0 + 1]))
        keep(a, rows, re, im)
    copies[4].wait()
    b[...] = dot_split(a, bwd)
    values = []
    for k0 in range(32):
        rows = slice(16 * k0, 16 * k0 + 16)
        values.append(
            cmul((b[rows, 0:128], b[rows, 128:256]), (twist[0, k0 : k0 + 1, :], -twist[1, k0 : k0 + 1, :]))
        )
    left = lax.broadcasted_iota(jnp.int32, (8, 128), 1) < 64
    for q, value in enumerate(fft(values, 1)):
        pixel, core = q // 4, (q // 2) % 2
        for half in range(2):
            parts = []
            for part in value:
                low, high = part[0:8], part[8:16]
                if half == 0:
                    parts.append(jnp.where(left, low, pltpu.roll(high, 64, 1)))
                else:
                    parts.append(jnp.where(left, pltpu.roll(low, 64, 1), high))
            message = jnp.concatenate(parts, axis=0).astype(BF16)
            block = 2 * (q % 2) + half
            for zh in range(2):
                y = (block + 2 * zh) % 4
                out[pixel * 16 + zh * 8 + y * 2 + core] = message


def compress_range(raw, phase):
    twist, fwd, bwd = range_tables()
    return pl.pallas_call(
        range_kernel,
        out_shape=jax.ShapeDtypeStruct((128, 16, 128), BF16),
        in_specs=[HBM] * 5,
        out_specs=VMEM,
        scratch_shapes=[
            pltpu.VMEM((2, 16, R), BF16),
            pltpu.VMEM((32, 128), F32),
            pltpu.VMEM((2, 32, 128), F32),
            pltpu.VMEM((768, 256), BF16),
            pltpu.VMEM((768, 256), BF16),
            pltpu.VMEM((512, 512), BF16),
            pltpu.VMEM((512, 256), F32),
            pltpu.SemaphoreType.DMA((5,)),
        ],
        compiler_params=params(24),
        cost_estimate=cost(4 * 10**8, 2 * 10**6, 8192),
        name="compress_range",
    )(*in_hbm(raw, phase.reshape(32, 128), *map(jnp.asarray, (twist, fwd, bwd))))


def prepare_kernel(angle_hbm, twist_hbm, mats_hbm, last_hbm, factors, mats, last, angle, sems):
    rows = archive_rows(0)
    copies = fetch(
        (angle_hbm.at[rows], twist_hbm, mats_hbm, last_hbm),
        (angle, factors.at[2:4], mats, last),
        sems,
    )
    copies[0].wait()
    for k in range(8):
        block = jnp.concatenate(
            [angle[:, 256 * k : 256 * k + 128], angle[:, 256 * k + 128 : 256 * k + 256]], axis=0
        )
        turned_block = block.astype(F32).T
        factors[0, k] = jnp.cos(turned_block) * (1.0 / A)
        factors[1, k] = jnp.sin(turned_block) * (1.0 / A)
    for copy in copies[1:]:
        copy.wait()


def prepare(azimuth_phase):
    tables = azimuth_tables()
    return pl.pallas_call(
        prepare_kernel,
        out_shape=(pltpu.VMEM((4, 8, 128, 128), F32), *(pltpu.VMEM(t.shape, t.dtype) for t in tables[1:])),
        in_specs=[HBM] * 4,
        out_specs=(VMEM,) * 3,
        scratch_shapes=[pltpu.VMEM((ROWS, A), BF16), pltpu.SemaphoreType.DMA((4,))],
        compiler_params=params(24),
        cost_estimate=cost(10**7, 8 * 10**6, 262144),
        name="prepare",
    )(*in_hbm(azimuth_phase, *map(jnp.asarray, tables)))


def focus_kernel(lines, factors, mats, last, out, wide, packed, spec, filtered, turned_rows, parts):
    wide[...] = lines[...].reshape(2048, 128).astype(F32)
    for j in range(16):
        ri, i = j // 8, j % 8
        packed[128 * ri : 128 * ri + 128, 128 * i : 128 * i + 128] = wide[pl.ds(j, 128, stride=16), :].astype(BF16)
    spec[...] = dot(mats[0:256, 0:256], packed[...]) + dot(mats[0:256, 256:512], packed[...])

    sign = jnp.where(lax.broadcasted_iota(jnp.int32, (8, 128), 1) < 64, 1.0, -1.0)

    def tile(step, carry):
        rows = pl.ds(pl.multiple_of(step * 8, 8), 8)
        below = pl.ds(pl.multiple_of(step * 8 + 128, 8), 8)
        values = []
        for i in range(8):
            lanes = slice(128 * i, 128 * i + 128)
            value = cmul((spec[rows, lanes], spec[below, lanes]), (factors[2, i, rows, :], factors[3, i, rows, :]))
            value = tuple(pltpu.roll(part, 64, 1) + part * sign for part in value)
            if i:
                value = cmul(value, (last[0, 16 + i : 17 + i, :], last[1, 16 + i : 17 + i, :]))
            values.append(value)
        for k, value in enumerate(fft(values, -1)):
            re, im = cmul(value, (factors[0, k, rows, :], factors[1, k, rows, :]))
            filtered[0, k, rows, :] = re
            filtered[1, k, rows, :] = im
        return carry

    lax.fori_loop(0, 16, tile, 0, unroll=True)

    for kappa in range(16):
        block = jnp.concatenate(
            [filtered[ri, k, pl.ds(kappa, 8, stride=16), :] for ri in range(2) for k in range(8)], axis=0
        )
        for n, part in enumerate(halves(block.T)):
            turned_rows[64 * kappa : 64 * kappa + 64, 256 * n : 256 * n + 128] = part[0:64]
            turned_rows[64 * kappa : 64 * kappa + 64, 256 * n + 128 : 256 * n + 256] = part[64:128]
    bwd_high, bwd_low = mats[256:512, 0:256], mats[256:512, 256:512]
    parts[...] = (
        dot(turned_rows[:, 0:256], bwd_high) + dot(turned_rows[:, 256:512], bwd_high) + dot(turned_rows[:, 0:256], bwd_low)
    )

    for step in range(4):
        rows = slice(16 * step, 16 * step + 16)
        values = []
        for kappa in range(16):
            here = slice(16 * step + 64 * kappa, 16 * step + 64 * kappa + 16)
            values.append(
                cmul(
                    (parts[here, 0:128], parts[here, 128:256]),
                    (last[0, kappa : kappa + 1, :], last[1, kappa : kappa + 1, :]),
                )
            )
        for alpha, (re, im) in enumerate(fft(values, 1)):
            lanes = slice(128 * alpha, 128 * alpha + 128)
            out[0, rows, lanes] = re.astype(BF16)
            out[1, rows, lanes] = im.astype(BF16)


def focus_columns(lines, factors, mats, last):
    return pl.pallas_call(
        focus_kernel,
        out_shape=jax.ShapeDtypeStruct((2, ROWS, A), BF16),
        in_specs=[VMEM] * 4,
        out_specs=VMEM,
        scratch_shapes=[
            pltpu.VMEM((2048, 128), F32),
            pltpu.VMEM((256, 1024), BF16),
            pltpu.VMEM((256, 1024), F32),
            pltpu.VMEM((2, 8, 128, 128), F32),
            pltpu.VMEM((1024, 512), BF16),
            pltpu.VMEM((1024, 256), F32),
        ],
        compiler_params=params(24),
        cost_estimate=cost(10**9, 4 * 10**6),
        name="focus_columns",
    )(lines, factors, mats, last)


def window_rows(pooled, row_count):
    return sum(pooled[pl.ds(j, row_count // 4, stride=4), :] for j in range(4)) * (1.0 / 64)


def inverse_root(power):
    return lax.rsqrt(power + EPSILON)


CHUNKS = [slice(256 * n, 256 * n + 256) for n in range(A // 256)]


def cross_products(products, row, image, old, old_rows):
    for lanes in CHUNKS:
        new_re, new_im = image[0, :, lanes], image[1, :, lanes]
        old_re, old_im = old[0, old_rows, lanes], old[1, old_rows, lanes]
        products[row : row + ROWS, lanes] = new_re * old_re + new_im * old_im
        products[row + ROWS : row + 2 * ROWS, lanes] = new_im * old_re - new_re * old_im


def power_products(products, row, image, rows):
    for lanes in CHUNKS:
        re, im = image[0, rows, lanes], image[1, rows, lanes]
        products[row : row + ROWS, lanes] = re * re + im * im


ALL_ROWS = slice(0, ROWS)


def block_rows(n):
    return slice(ROWS * n, ROWS * n + ROWS)


def pool(products, pooling, pooled, count):
    pooled[0 : count * ROWS, :] = dot(products[0 : count * ROWS, :], pooling[...])
    return window_rows(pooled.at[0 : count * ROWS], count * ROWS).reshape(count, 16, 128)


def scratch(count):
    return [pltpu.VMEM((count * ROWS, A), BF16), pltpu.VMEM((count * ROWS, 128), F32)]


def first_kernel(
    image, own, other, pooling_hbm, first, held, old_scales, pooling, here, products, pooled, sems
):
    copies = []
    for n in range(4):
        rows = archive_rows(n)
        for m, source in enumerate((own, other)):
            if n == 0:
                target = here.at[2 * m : 2 * m + 2]
            else:
                target = held.at[2 * m : 2 * m + 2, :, block_rows(n - 1)]
            copies.append(pltpu.make_async_copy(source.at[:, :, rows], target, sems.at[2 * n + m]))
            copies[-1].start()
    copies.append(pltpu.make_async_copy(pooling_hbm, pooling, sems.at[8]))
    copies[-1].start()
    power_products(products, 12 * ROWS, image, ALL_ROWS)
    copies[0].wait()
    copies[1].wait()
    for date in range(4):
        cross_products(products, 2 * date * ROWS, image, here.at[date], ALL_ROWS)
        power_products(products, (8 + date) * ROWS, here.at[date], ALL_ROWS)
    copies[8].wait()
    sums = pool(products, pooling, pooled, 13)
    new = inverse_root(sums[12])
    for date in range(4):
        scale = new * inverse_root(sums[8 + date])
        for part in range(2):
            first[date, part] = sums[2 * date + part] * scale
    for n in range(1, 4):
        copies[2 * n].wait()
        copies[2 * n + 1].wait()
        for date in range(4):
            power_products(products, date * ROWS, held.at[date], block_rows(n - 1))
        old_scales[n - 1] = inverse_root(pool(products, pooling, pooled, 4))


def cross_first(image, own, other, pooling):
    return pl.pallas_call(
        first_kernel,
        out_shape=(
            jax.ShapeDtypeStruct((4, 2, 16, 128), F32),
            pltpu.VMEM((4, 2, 3 * ROWS, A), BF16),
            jax.ShapeDtypeStruct((3, 4, 16, 128), F32),
            pltpu.VMEM((A, 128), BF16),
        ),
        in_specs=[VMEM, HBM, HBM, HBM],
        out_specs=(VMEM,) * 4,
        scratch_shapes=[pltpu.VMEM((4, 2, ROWS, A), BF16), *scratch(13), pltpu.SemaphoreType.DMA((9,))],
        compiler_params=params(24),
        cost_estimate=cost(10**9, 8 * 10**6),
        name="cross_first",
    )(image, *in_hbm(own, other, pooling))


def block_kernel(n, image, held, old_scales, pooling, out, products, pooled):
    for date in range(4):
        cross_products(products, 2 * date * ROWS, image, held.at[date], block_rows(n))
    power_products(products, 8 * ROWS, image, ALL_ROWS)
    sums = pool(products, pooling, pooled, 9)
    new = inverse_root(sums[8])
    for date in range(4):
        scale = new * old_scales[n, date]
        for part in range(2):
            out[date, part] = sums[2 * date + part] * scale


def cross_block(n, image, held, old_scales, pooling):
    return pl.pallas_call(
        partial(block_kernel, n),
        out_shape=jax.ShapeDtypeStruct((4, 2, 16, 128), F32),
        in_specs=[VMEM] * 4,
        out_specs=VMEM,
        scratch_shapes=scratch(9),
        compiler_params=params(24),
        cost_estimate=cost(10**8, 4 * 10**6),
        name="cross_block",
    )(image, held, old_scales, pooling)


def put(n, target, parts):
    target[:, :, pl.ds(pl.multiple_of(place()[1][n] * 16, 16), 16), :] = parts


def other_kernel(image1, image2, held, old_scales, pooling, part0, part1, out, new_scale, products, pooled):
    for n, image in enumerate((image1, image2)):
        for date in range(2):
            cross_products(products, (4 * n + 2 * date) * ROWS, image, held.at[2 + date], block_rows(n + 1))
        power_products(products, (8 + n) * ROWS, image, ALL_ROWS)
    for n, part in enumerate((part0, part1)):
        put(n, out, part[2:4])
    sums = pool(products, pooling, pooled, 10)
    for n in range(2):
        new = inverse_root(sums[8 + n])
        new_scale[n] = new
        put(n + 2, out, sums[4 * n : 4 * n + 4].reshape(2, 2, 16, 128) * (new * old_scales[n + 1, 2:4])[:, None])


def cross_others(images, held, old_scales, pooling, parts):
    return pl.pallas_call(
        other_kernel,
        out_shape=(jax.ShapeDtypeStruct((2, 2, 64, 128), F32), jax.ShapeDtypeStruct((2, 16, 128), F32)),
        in_specs=[VMEM] * 7,
        out_specs=(VMEM, VMEM),
        scratch_shapes=scratch(10),
        compiler_params=params(24),
        cost_estimate=cost(10**8, 4 * 10**6),
        name="cross_others",
    )(*images, held, old_scales, pooling, *parts)


def own_kernel(image1, image2, held, old_scales, pooling, part0, part1, new_scale, out, products, pooled):
    for n, image in enumerate((image1, image2)):
        for date in range(2):
            cross_products(products, (4 * n + 2 * date) * ROWS, image, held.at[date], block_rows(n + 1))
    for n, part in enumerate((part0, part1)):
        put(n, out, part[0:2])
    sums = pool(products, pooling, pooled, 8)
    for n in range(2):
        scale = (new_scale[n] * old_scales[n + 1, 0:2])[:, None]
        put(n + 2, out, sums[4 * n : 4 * n + 4].reshape(2, 2, 16, 128) * scale)


def cross_own(images, held, old_scales, pooling, parts, new_scale):
    return pl.pallas_call(
        own_kernel,
        out_shape=jax.ShapeDtypeStruct((2, 2, 64, 128), F32),
        in_specs=[VMEM] * 8,
        out_specs=VMEM,
        scratch_shapes=scratch(8),
        compiler_params=params(24),
        cost_estimate=cost(10**8, 4 * 10**6),
        name="cross_own",
    )(*images, held, old_scales, pooling, *parts, new_scale)


def final_kernel(order, mine, received, out):
    core, _ = place()
    odd_first = order[...] & 1 == 1
    for half, source in ((core, mine), (1 - core, received)):
        rows = pl.ds(pl.multiple_of(half * 64, 64), 64)
        for part in range(2):
            even, odd = source[0, part], source[1, part]
            out[0, part, rows, :] = jnp.where(odd_first, odd, even)
            out[1, part, rows, :] = jnp.where(odd_first, even, odd)


def assemble(date_order, mine, received):
    return pl.pallas_call(
        final_kernel,
        out_shape=jax.ShapeDtypeStruct((2, 2, 128, 128), F32),
        in_specs=[VMEM] * 3,
        out_specs=VMEM,
        compiler_params=params(24),
        cost_estimate=cost(10**6, 10**6),
        name="assemble",
    )(jnp.broadcast_to(date_order[0], (1, 128)), mine, received)


def pairs(step):
    out = []
    for date in range(16):
        zh, y, core = step(date // 8, date // 2 % 4, date % 2)
        out.append((date, zh * 8 + y % 4 * 2 + core))
    return out


OTHER_CORE = pairs(lambda zh, y, core: (zh, y, 1 - core))
ROUNDS = (
    pairs(lambda zh, y, core: (zh, y + 3, core) if core else (zh, y + 1, core)),
    pairs(lambda zh, y, core: (1 - zh, y, core)),
    pairs(lambda zh, y, core: (zh, y + 1, core) if core else (zh, y + 3, core)),
)


def on_device(raw_echoes, range_phase, azimuth_phase, archive, date_order):
    messages = compress_range(raw_echoes, range_phase)
    messages, azimuth_phase, archive = lax.optimization_barrier((messages, azimuth_phase, archive))
    lines = lax.all_to_all(messages, ALL, 0, 0, tiled=True)
    other_archive = lax.ppermute(archive, "date", OTHER_CORE)
    image = focus_columns(lines, *prepare(azimuth_phase))
    images = [lax.ppermute(image, "date", perm) for perm in ROUNDS]
    first, *kept = cross_first(image, archive, other_archive, jnp.asarray(pooling_table()))
    parts = [first, cross_block(0, images[0], *kept)]
    others, new_scale = cross_others(images[1:], *kept, parts)
    received = lax.ppermute(others, "date", OTHER_CORE)
    mine = cross_own(images[1:], *kept, parts, new_scale)
    return assemble(date_order, mine, received)


def solution(mesh):
    return jax.shard_map(
        on_device,
        mesh=mesh,
        in_specs=(P(None, ALL, None), P(), P("pixel", None), P("date", None, "pixel", None), P("date")),
        out_specs=P("date", None, "pixel", None),
        check_vma=False,
    )
```

```python
from functools import partial
import math

import jax
import jax.numpy as jnp
import numpy as np
from jax import lax
from jax.experimental import pallas as pl
from jax.experimental.pallas import tpu as pltpu
from jax.sharding import PartitionSpec as P

F32 = jnp.float32
BF16 = jnp.bfloat16
EPSILON = 1e-06
R = 4096
A = 2048
ROWS = 64
LINES = 16
ALL = ("pixel", "date")
VMEM = pl.BlockSpec(memory_space=pltpu.VMEM)
HBM = pl.BlockSpec(memory_space=pltpu.HBM)


def cmul(a, b):
    return (a[0] * b[0] - a[1] * b[1], a[0] * b[1] + a[1] * b[0])


def turned(value, k, n, sign):
    if k == 0:
        return value
    re, im = value
    if 8 * k == n:
        return ((re - im) * math.sqrt(0.5), (im + re) * math.sqrt(0.5)) if sign > 0 else (
            (re + im) * math.sqrt(0.5),
            (im - re) * math.sqrt(0.5),
        )
    if 8 * k == 3 * n:
        return ((re + im) * -math.sqrt(0.5), (re - im) * math.sqrt(0.5)) if sign > 0 else (
            (im - re) * math.sqrt(0.5),
            (re + im) * -math.sqrt(0.5),
        )
    angle = sign * 2.0 * math.pi * k / n
    return cmul(value, (math.cos(angle), math.sin(angle)))


def fft(values, sign):
    n = len(values)
    if n == 1:
        return values
    even, odd = fft(values[0::2], sign), fft(values[1::2], sign)
    low, high = [], []
    for k in range(n // 2):
        er, ei = even[k]
        if 4 * k == n:
            tr, ti = odd[k]
            plus, minus = (er - ti, ei + tr), (er + ti, ei - tr)
            low.append(plus if sign > 0 else minus)
            high.append(minus if sign > 0 else plus)
        else:
            tr, ti = turned(odd[k], k, n, sign)
            low.append((er + tr, ei + ti))
            high.append((er - tr, ei - ti))
    return low + high


def split(table):
    table = np.asarray(table, np.float32)
    high = table.astype(BF16)
    low = (table - high.astype(np.float32)).astype(BF16)
    return high, low


def real_form(angle, sign):
    c, s = np.cos(angle), sign * np.sin(angle)
    return np.block([[c, s], [-s, c]])


def range_tables():
    t = np.arange(128)
    k1 = 4 * (t % 32) + t // 32
    angle = 2 * np.pi * np.outer(t, k1) / 128
    fwd, bwd = (
        np.concatenate([high, high, low], axis=0)
        for high, low in (split(real_form(angle, -1)), split(real_form(angle.T, 1)))
    )
    twist = 2 * np.pi * np.outer(np.arange(32), t) / R
    return np.stack([np.cos(twist), -np.sin(twist)]).astype(np.float32), fwd, bwd


def azimuth_tables():
    s = np.arange(128)
    fwd = np.concatenate(split(real_form(2 * np.pi * np.outer(s, s) / 128, -1).T), axis=1)
    k1 = np.arange(128)[:, None]
    i = np.arange(8)[None, :]
    twist = np.stack([np.exp(-2j * np.pi * (i + 8 * half) * k1 / A) for half in (0, 1)], axis=-1)
    twist = np.repeat(np.stack([twist.real, twist.imag]), 64, axis=-1).transpose(0, 2, 1, 3).astype(np.float32)
    odd = np.exp(-2j * np.pi * np.arange(8)[:, None] / 16 * (np.arange(128)[None, :] // 64))
    k, lam = np.meshgrid(np.arange(8), np.arange(8), indexing="ij")
    m = (lam + 16 * k).reshape(64)
    beta = np.arange(128)
    parts = [real_form(2 * np.pi * np.outer(m + 8 * par, beta) / 128, 1) for par in (0, 1)]
    bwd = np.concatenate(split(np.concatenate(parts, axis=0)), axis=1)
    last = 2 * np.pi * np.outer(np.arange(16), beta) / A
    rows = np.concatenate([np.exp(1j * last), odd], axis=0)
    rows = np.stack([rows.real, rows.imag]).astype(np.float32)
    return twist, np.concatenate([fwd, bwd], axis=0), rows


def pooling_table():
    return (np.arange(A)[:, None] // 16 == np.arange(128)[None, :]).astype(BF16)


def dot(a, b):
    return jnp.dot(a, b, preferred_element_type=F32)


def halves(x):
    high = x.astype(BF16)
    return high, (x - high.astype(F32)).astype(BF16)


def keep(target, rows, re, im):
    (re_high, re_low), (im_high, im_low) = halves(re), halves(im)
    target[rows, 0:128] = re_high
    target[rows, 128:256] = im_high
    target[rows, 256:384] = re_low
    target[rows, 384:512] = im_low


def dot_split(x, table):
    return dot(x[...], table[0:512]) + dot(x[:, 0:256], table[512:768])


def params(mib):
    return pltpu.CompilerParams(vmem_limit_bytes=mib * 2**20)


def cost(flops, moved, transcendentals=0):
    return pl.CostEstimate(flops=flops, bytes_accessed=moved, transcendentals=transcendentals)


def in_hbm(*arrays):
    return [pltpu.with_memory_space_constraint(x, pltpu.HBM) for x in arrays]


def in_vmem(*arrays):
    return [pltpu.with_memory_space_constraint(x, pltpu.VMEM) for x in arrays]


def fetch(sources, targets, sems):
    copies = [
        pltpu.make_async_copy(source, target, sems.at[n]) for n, (source, target) in enumerate(zip(sources, targets))
    ]
    for copy in copies:
        copy.start()
    return copies


def place():
    date = lax.axis_index("date")
    zh, y, core = lax.shift_right_logical(date, 3), lax.shift_right_logical(date, 1) & 3, date & 1
    block = (y + 2 * zh) & 3
    return core, (block, (block + 3) & 3, (block + 2) & 3, (block + 1) & 3)


def archive_rows(n):
    core, blocks = place()
    return pl.ds(pl.multiple_of((4 * core + blocks[n]) * ROWS, ROWS), ROWS)


def range_kernel(raw_hbm, phase_hbm, twist_hbm, fwd_hbm, bwd_hbm, out, raw, phase, twist, fwd, bwd, a, b, sems):
    copies = fetch(
        (phase_hbm, raw_hbm, twist_hbm, fwd_hbm, bwd_hbm), (phase, raw, twist, fwd, bwd), sems
    )
    copies[0].wait()
    angle = phase[...]
    angle = jnp.concatenate(
        [angle] + [pltpu.roll(angle, 128 - 32 * g, 1) for g in range(1, 4)], axis=0
    ).T[0:32]
    cosine, sine = jnp.cos(angle) * (1.0 / R), jnp.sin(angle) * (1.0 / R)
    copies[1].wait()
    copies[2].wait()
    values = [
        (raw[0, :, 128 * q : 128 * q + 128].astype(F32), raw[1, :, 128 * q : 128 * q + 128].astype(F32))
        for q in range(32)
    ]
    for k0, value in enumerate(fft(values, -1)):
        re, im = cmul(value, (twist[0, k0 : k0 + 1, :], twist[1, k0 : k0 + 1, :]))
        keep(a, slice(16 * k0, 16 * k0 + 16), re, im)
    copies[3].wait()
    b[...] = dot_split(a, fwd)
    for k0 in range(32):
        rows = slice(16 * k0, 16 * k0 + 16)
        re, im = cmul((b[rows, 0:128], b[rows, 128:256]), (cosine[k0 : k0 + 1], sine[k0 : k0 + 1]))
        keep(a, rows, re, im)
    copies[4].wait()
    b[...] = dot_split(a, bwd)
    values = []
    for k0 in range(32):
        rows = slice(16 * k0, 16 * k0 + 16)
        values.append(
            cmul((b[rows, 0:128], b[rows, 128:256]), (twist[0, k0 : k0 + 1, :], -twist[1, k0 : k0 + 1, :]))
        )
    left = lax.broadcasted_iota(jnp.int32, (8, 128), 1) < 64
    for q, value in enumerate(fft(values, 1)):
        pixel, core = q // 4, (q // 2) % 2
        for half in range(2):
            parts = []
            for part in value:
                low, high = part[0:8], part[8:16]
                if half == 0:
                    parts.append(jnp.where(left, low, pltpu.roll(high, 64, 1)))
                else:
                    parts.append(jnp.where(left, pltpu.roll(low, 64, 1), high))
            message = jnp.concatenate(parts, axis=0).astype(BF16)
            block = 2 * (q % 2) + half
            for zh in range(2):
                y = (block + 2 * zh) % 4
                out[pixel * 16 + zh * 8 + y * 2 + core] = message


def compress_range(raw, phase):
    twist, fwd, bwd = range_tables()
    return pl.pallas_call(
        range_kernel,
        out_shape=jax.ShapeDtypeStruct((128, 16, 128), BF16),
        in_specs=[HBM] * 5,
        out_specs=VMEM,
        scratch_shapes=[
            pltpu.VMEM((2, 16, R), BF16),
            pltpu.VMEM((32, 128), F32),
            pltpu.VMEM((2, 32, 128), F32),
            pltpu.VMEM((768, 256), BF16),
            pltpu.VMEM((768, 256), BF16),
            pltpu.VMEM((512, 512), BF16),
            pltpu.VMEM((512, 256), F32),
            pltpu.SemaphoreType.DMA((5,)),
        ],
        compiler_params=params(24),
        cost_estimate=cost(4 * 10**8, 2 * 10**6, 8192),
        name="compress_range",
    )(*in_hbm(raw, phase.reshape(32, 128), *map(jnp.asarray, (twist, fwd, bwd))))


def prepare_kernel(angle_hbm, twist_hbm, mats_hbm, last_hbm, factors, mats, last, angle, sems):
    rows = archive_rows(0)
    copies = fetch(
        (angle_hbm.at[rows], twist_hbm, mats_hbm, last_hbm),
        (angle, factors.at[2:4], mats, last),
        sems,
    )
    copies[0].wait()
    for k in range(8):
        block = jnp.concatenate(
            [angle[:, 256 * k : 256 * k + 128], angle[:, 256 * k + 128 : 256 * k + 256]], axis=0
        )
        turned_block = block.astype(F32).T
        factors[0, k] = jnp.cos(turned_block) * (1.0 / A)
        factors[1, k] = jnp.sin(turned_block) * (1.0 / A)
    for copy in copies[1:]:
        copy.wait()


def prepare(azimuth_phase):
    tables = azimuth_tables()
    return pl.pallas_call(
        prepare_kernel,
        out_shape=(pltpu.VMEM((4, 8, 128, 128), F32), *(pltpu.VMEM(t.shape, t.dtype) for t in tables[1:])),
        in_specs=[HBM] * 4,
        out_specs=(VMEM,) * 3,
        scratch_shapes=[pltpu.VMEM((ROWS, A), BF16), pltpu.SemaphoreType.DMA((4,))],
        compiler_params=params(24),
        cost_estimate=cost(10**7, 8 * 10**6, 262144),
        name="prepare",
    )(*in_hbm(azimuth_phase, *map(jnp.asarray, tables)))


def focus_kernel(lines, factors, mats, last, out, wide, packed, spec, filtered, turned_rows, parts):
    wide[...] = lines[...].reshape(2048, 128).astype(F32)
    for j in range(16):
        ri, i = j // 8, j % 8
        packed[128 * ri : 128 * ri + 128, 128 * i : 128 * i + 128] = wide[pl.ds(j, 128, stride=16), :].astype(BF16)
    spec[...] = dot(mats[0:256, 0:256], packed[...]) + dot(mats[0:256, 256:512], packed[...])

    sign = jnp.where(lax.broadcasted_iota(jnp.int32, (8, 128), 1) < 64, 1.0, -1.0)

    def tile(step, carry):
        rows = pl.ds(pl.multiple_of(step * 8, 8), 8)
        below = pl.ds(pl.multiple_of(step * 8 + 128, 8), 8)
        values = []
        for i in range(8):
            lanes = slice(128 * i, 128 * i + 128)
            value = cmul((spec[rows, lanes], spec[below, lanes]), (factors[2, i, rows, :], factors[3, i, rows, :]))
            value = tuple(pltpu.roll(part, 64, 1) + part * sign for part in value)
            if i:
                value = cmul(value, (last[0, 16 + i : 17 + i, :], last[1, 16 + i : 17 + i, :]))
            values.append(value)
        for k, value in enumerate(fft(values, -1)):
            re, im = cmul(value, (factors[0, k, rows, :], factors[1, k, rows, :]))
            filtered[0, k, rows, :] = re
            filtered[1, k, rows, :] = im
        return carry

    lax.fori_loop(0, 16, tile, 0, unroll=True)

    for kappa in range(16):
        block = jnp.concatenate(
            [filtered[ri, k, pl.ds(kappa, 8, stride=16), :] for ri in range(2) for k in range(8)], axis=0
        )
        for n, part in enumerate(halves(block.T)):
            turned_rows[64 * kappa : 64 * kappa + 64, 256 * n : 256 * n + 128] = part[0:64]
            turned_rows[64 * kappa : 64 * kappa + 64, 256 * n + 128 : 256 * n + 256] = part[64:128]
    bwd_high, bwd_low = mats[256:512, 0:256], mats[256:512, 256:512]
    parts[...] = (
        dot(turned_rows[:, 0:256], bwd_high) + dot(turned_rows[:, 256:512], bwd_high) + dot(turned_rows[:, 0:256], bwd_low)
    )

    for step in range(4):
        rows = slice(16 * step, 16 * step + 16)
        values = []
        for kappa in range(16):
            here = slice(16 * step + 64 * kappa, 16 * step + 64 * kappa + 16)
            values.append(
                cmul(
                    (parts[here, 0:128], parts[here, 128:256]),
                    (last[0, kappa : kappa + 1, :], last[1, kappa : kappa + 1, :]),
                )
            )
        for alpha, (re, im) in enumerate(fft(values, 1)):
            lanes = slice(128 * alpha, 128 * alpha + 128)
            out[0, rows, lanes] = re.astype(BF16)
            out[1, rows, lanes] = im.astype(BF16)


def focus_columns(lines, factors, mats, last):
    return pl.pallas_call(
        focus_kernel,
        out_shape=jax.ShapeDtypeStruct((2, ROWS, A), BF16),
        in_specs=[VMEM] * 4,
        out_specs=VMEM,
        scratch_shapes=[
            pltpu.VMEM((2048, 128), F32),
            pltpu.VMEM((256, 1024), BF16),
            pltpu.VMEM((256, 1024), F32),
            pltpu.VMEM((2, 8, 128, 128), F32),
            pltpu.VMEM((1024, 512), BF16),
            pltpu.VMEM((1024, 256), F32),
        ],
        compiler_params=params(24),
        cost_estimate=cost(10**9, 4 * 10**6),
        name="focus_columns",
    )(lines, factors, mats, last)


def window_rows(pooled, row_count):
    return sum(pooled[pl.ds(j, row_count // 4, stride=4), :] for j in range(4)) * (1.0 / 64)


def inverse_root(power):
    return lax.rsqrt(power + EPSILON)


CHUNKS = [slice(256 * n, 256 * n + 256) for n in range(A // 256)]


def cross_products(products, row, image, old, old_rows):
    for lanes in CHUNKS:
        new_re, new_im = image[0, :, lanes], image[1, :, lanes]
        old_re, old_im = old[0, old_rows, lanes], old[1, old_rows, lanes]
        products[row : row + ROWS, lanes] = new_re * old_re + new_im * old_im
        products[row + ROWS : row + 2 * ROWS, lanes] = new_im * old_re - new_re * old_im


def power_products(products, row, image, rows):
    for lanes in CHUNKS:
        re, im = image[0, rows, lanes], image[1, rows, lanes]
        products[row : row + ROWS, lanes] = re * re + im * im


ALL_ROWS = slice(0, ROWS)


def block_rows(n):
    return slice(ROWS * n, ROWS * n + ROWS)


def pool(products, pooling, pooled, count):
    pooled[0 : count * ROWS, :] = dot(products[0 : count * ROWS, :], pooling[...])
    return window_rows(pooled.at[0 : count * ROWS], count * ROWS).reshape(count, 16, 128)


def scratch(count):
    return [pltpu.VMEM((count * ROWS, A), BF16), pltpu.VMEM((count * ROWS, 128), F32)]


def first_kernel(
    image, own, other, pooling_hbm, first, held, old_scales, pooling, here, products, pooled, sems
):
    copies = []
    for n in range(4):
        rows = archive_rows(n)
        for m, source in enumerate((own, other)):
            if n == 0:
                target = here.at[2 * m : 2 * m + 2]
            else:
                target = held.at[2 * m : 2 * m + 2, :, block_rows(n - 1)]
            copies.append(pltpu.make_async_copy(source.at[:, :, rows], target, sems.at[2 * n + m]))
            copies[-1].start()
    copies.append(pltpu.make_async_copy(pooling_hbm, pooling, sems.at[8]))
    copies[-1].start()
    power_products(products, 12 * ROWS, image, ALL_ROWS)
    copies[0].wait()
    copies[1].wait()
    for date in range(4):
        cross_products(products, 2 * date * ROWS, image, here.at[date], ALL_ROWS)
        power_products(products, (8 + date) * ROWS, here.at[date], ALL_ROWS)
    copies[8].wait()
    sums = pool(products, pooling, pooled, 13)
    new = inverse_root(sums[12])
    for date in range(4):
        scale = new * inverse_root(sums[8 + date])
        for part in range(2):
            first[date, part] = sums[2 * date + part] * scale
    for n in range(1, 4):
        copies[2 * n].wait()
        copies[2 * n + 1].wait()
        for date in range(4):
            power_products(products, date * ROWS, held.at[date], block_rows(n - 1))
        old_scales[n - 1] = inverse_root(pool(products, pooling, pooled, 4))


def cross_first(image, own, other, pooling):
    return pl.pallas_call(
        first_kernel,
        out_shape=(
            jax.ShapeDtypeStruct((4, 2, 16, 128), F32),
            pltpu.VMEM((4, 2, 3 * ROWS, A), BF16),
            jax.ShapeDtypeStruct((3, 4, 16, 128), F32),
            pltpu.VMEM((A, 128), BF16),
        ),
        in_specs=[VMEM, HBM, HBM, HBM],
        out_specs=(VMEM,) * 4,
        scratch_shapes=[pltpu.VMEM((4, 2, ROWS, A), BF16), *scratch(13), pltpu.SemaphoreType.DMA((9,))],
        compiler_params=params(24),
        cost_estimate=cost(10**9, 8 * 10**6),
        name="cross_first",
    )(image, *in_hbm(own, other, pooling))


def block_kernel(n, image, held, old_scales, pooling, out, products, pooled):
    for date in range(4):
        cross_products(products, 2 * date * ROWS, image, held.at[date], block_rows(n))
    power_products(products, 8 * ROWS, image, ALL_ROWS)
    sums = pool(products, pooling, pooled, 9)
    new = inverse_root(sums[8])
    for date in range(4):
        scale = new * old_scales[n, date]
        for part in range(2):
            out[date, part] = sums[2 * date + part] * scale


def cross_block(n, image, held, old_scales, pooling):
    return pl.pallas_call(
        partial(block_kernel, n),
        out_shape=jax.ShapeDtypeStruct((4, 2, 16, 128), F32),
        in_specs=[VMEM] * 4,
        out_specs=VMEM,
        scratch_shapes=scratch(9),
        compiler_params=params(24),
        cost_estimate=cost(10**8, 4 * 10**6),
        name="cross_block",
    )(image, held, old_scales, pooling)


def put(n, target, parts):
    target[:, :, pl.ds(pl.multiple_of(place()[1][n] * 16, 16), 16), :] = parts


def other_kernel(image1, image2, held, old_scales, pooling, part0, part1, out, new_scale, products, pooled):
    for n, image in enumerate((image1, image2)):
        for date in range(2):
            cross_products(products, (4 * n + 2 * date) * ROWS, image, held.at[2 + date], block_rows(n + 1))
        power_products(products, (8 + n) * ROWS, image, ALL_ROWS)
    for n, part in enumerate((part0, part1)):
        put(n, out, part[2:4])
    sums = pool(products, pooling, pooled, 10)
    for n in range(2):
        new = inverse_root(sums[8 + n])
        new_scale[n] = new
        put(n + 2, out, sums[4 * n : 4 * n + 4].reshape(2, 2, 16, 128) * (new * old_scales[n + 1, 2:4])[:, None])


def cross_others(images, held, old_scales, pooling, parts):
    return pl.pallas_call(
        other_kernel,
        out_shape=(jax.ShapeDtypeStruct((2, 2, 64, 128), F32), jax.ShapeDtypeStruct((2, 16, 128), F32)),
        in_specs=[VMEM] * 7,
        out_specs=(VMEM, VMEM),
        scratch_shapes=scratch(10),
        compiler_params=params(24),
        cost_estimate=cost(10**8, 4 * 10**6),
        name="cross_others",
    )(*images, held, old_scales, pooling, *parts)


def own_kernel(image1, image2, held, old_scales, pooling, part0, part1, new_scale, out, products, pooled):
    for n, image in enumerate((image1, image2)):
        for date in range(2):
            cross_products(products, (4 * n + 2 * date) * ROWS, image, held.at[date], block_rows(n + 1))
    for n, part in enumerate((part0, part1)):
        put(n, out, part[0:2])
    sums = pool(products, pooling, pooled, 8)
    for n in range(2):
        scale = (new_scale[n] * old_scales[n + 1, 0:2])[:, None]
        put(n + 2, out, sums[4 * n : 4 * n + 4].reshape(2, 2, 16, 128) * scale)


def cross_own(images, held, old_scales, pooling, parts, new_scale):
    return pl.pallas_call(
        own_kernel,
        out_shape=jax.ShapeDtypeStruct((2, 2, 64, 128), F32),
        in_specs=[VMEM] * 8,
        out_specs=VMEM,
        scratch_shapes=scratch(8),
        compiler_params=params(24),
        cost_estimate=cost(10**8, 4 * 10**6),
        name="cross_own",
    )(*images, held, old_scales, pooling, *parts, new_scale)


def final_kernel(order, mine, received, out):
    core, _ = place()
    odd_first = order[...] & 1 == 1
    for half, source in ((core, mine), (1 - core, received)):
        rows = pl.ds(pl.multiple_of(half * 64, 64), 64)
        for part in range(2):
            even, odd = source[0, part], source[1, part]
            out[0, part, rows, :] = jnp.where(odd_first, odd, even)
            out[1, part, rows, :] = jnp.where(odd_first, even, odd)


def assemble(order_row, mine, received):
    return pl.pallas_call(
        final_kernel,
        out_shape=jax.ShapeDtypeStruct((2, 2, 128, 128), F32),
        in_specs=[VMEM] * 3,
        out_specs=VMEM,
        compiler_params=params(24),
        cost_estimate=cost(10**6, 10**6),
        name="assemble",
    )(order_row, mine, received)


def pairs(step):
    out = []
    for date in range(16):
        zh, y, core = step(date // 8, date // 2 % 4, date % 2)
        out.append((date, zh * 8 + y % 4 * 2 + core))
    return out


OTHER_CORE = pairs(lambda zh, y, core: (zh, y, 1 - core))
OTHER_Z = pairs(lambda zh, y, core: (1 - zh, y, core))
NEXT_Y = pairs(lambda zh, y, core: (zh, y + 1, core))
LAST_Y = pairs(lambda zh, y, core: (zh, y + 3, core))


def on_device(raw_echoes, range_phase, azimuth_phase, archive, date_order):
    messages = compress_range(raw_echoes, range_phase)
    messages, azimuth_phase, archive = lax.optimization_barrier((messages, azimuth_phase, archive))
    lines = lax.all_to_all(messages, ALL, 0, 0, tiled=True)
    other_archive = lax.ppermute(archive, "date", OTHER_CORE)
    image = focus_columns(lines, *prepare(azimuth_phase))
    images = [lax.ppermute(image, "date", perm) for perm in (NEXT_Y, OTHER_Z, LAST_Y)]
    first, *kept = cross_first(image, archive, other_archive, jnp.asarray(pooling_table()))
    first, order_row = lax.optimization_barrier((first, jnp.broadcast_to(date_order[0], (1, 128))))
    parts = [first, cross_block(0, images[0], *kept)]
    others, new_scale = cross_others(images[1:], *kept, parts)
    received = lax.ppermute(others, "date", OTHER_CORE)
    mine = cross_own(images[1:], *kept, parts, new_scale)
    return assemble(order_row, mine, received)


def solution(mesh):
    return jax.shard_map(
        on_device,
        mesh=mesh,
        in_specs=(P(None, ALL, None), P(), P("pixel", None), P("date", None, "pixel", None), P("date")),
        out_specs=P("date", None, "pixel", None),
        check_vma=False,
    )
```
